32 devices in a mesh: groups: 2 (over y), pb: 4 (over x, core), ka: 4 (over z).
Axes of the slice: x: 2, y: 2, z: 4, core: 2. Of those that a mesh axis runs over, the one named last changes fastest.
Arguments:
- queries: bfloat16 [4096, 2048], P(('groups', 'pb')), parts along dimension 0, may hold values from -6 to 6
- keys: bfloat16 [4096, 2048], P(('groups', 'ka'), 'pb'), parts along dimension 0, may hold values from -6 to 6
- values: bfloat16 [4096, 2048], P(('groups', 'ka'), 'pb'), parts along dimension 0, may hold values from -6 to 6
- step_of: int32 [4096], P('groups'), parts along dimension 0, may hold values from 0 to 255, never falling along the last dimension, each value on 1 to 16 neighbouring positions
Outputs:
- attended: bfloat16 [4096, 2048], P(('groups', 'pb', 'ka')), parts along dimension 0
The draws below stay inside these ranges and needn't reach their ends.
There are 2 independent parts, one for each index of `groups`. The reference program is written for one: setup_inputs(seed, part) draws one part's arguments, and reference() takes and returns one part's arrays. A program takes and returns all parts, laid end to end along the dimension named above; each array names one. Nothing has to cross between parts.
Inputs may be any that keep to these rules, and one draw needn't show every extreme that they name: `step_of`: never falling along the episode; a step holds 1 to 16 tokens, one step exactly 16.
All inputs are finite; a program needn't handle non-finite values.
Results may differ from the reference program's by a relative error of at most 0.015.
Values may be sent and summed in bfloat16 or wider, within the bound.
No kernel may reach another device: no remote copies, remote signals or barrier semaphores. Data moves between devices by JAX's collectives and lax.ppermute only.
A program may use at most 64 MiB of HBM per device.

```python
import math
import jax
import jax.numpy as jnp
import numpy as np
from jax import lax

HEADS = 16
HEAD_DIM = 128
MOST = 16
SEQ = 2048
STEPS = 256


def draw_queries(key, part):
    field_key = jax.random.fold_in(key, 1)
    field = 1.75 * jax.random.truncated_normal(field_key, -3.4, 3.4, (SEQ, HEADS * HEAD_DIM), jnp.float32)
    return field.astype(jnp.bfloat16)


def draw_keys(key, part):
    field_key = jax.random.fold_in(key, 2)
    field = 1.75 * jax.random.truncated_normal(field_key, -3.4, 3.4, (SEQ, HEADS * HEAD_DIM), jnp.float32)
    return field.astype(jnp.bfloat16)


def block_scale(key, dims, cuts, smallest, largest):
    loudness, own = 1.0, jax.random.fold_in(key, 6)
    for position, parts in cuts:
        draws = jnp.exp(jax.random.uniform(jax.random.fold_in(own, position), (parts,), jnp.float32, smallest / len(cuts), largest / len(cuts)))
        loudness = loudness * jnp.repeat(draws, dims[position] // parts).reshape([-1 if axis == position else 1 for axis in range(len(dims))])
    return loudness


def profile(count, total, bound, skew):
    loads = [(1 << 20) // math.isqrt(grade ** skew) + 1 for grade in range(2, count + 1)]
    rest, counts = total - bound - (count - 1), [1] * (count - 1)
    while rest > 0:
        candidates = [i for i in range(count - 1) if counts[i] < bound]
        pool, budget = sum([loads[i] for i in candidates]), rest
        for i in candidates:
            addition = min(bound - counts[i], max(1, budget * loads[i] // pool), rest)
            counts[i] = counts[i] + addition
            rest = rest - addition
    return np.array([bound] + counts)


def ragged_sizes(stream_key, count, total, limit, skew):
    if count == 2:
        one = jax.random.randint(stream_key, (), max(1, total - limit), min(limit, total - 1) + 1)
        return jnp.stack([one, total - one])
    lengths = jnp.asarray(profile(count, total, limit, skew), jnp.int32)
    pairs = (count - 1) // 2
    source_of, taker = lengths[1:1 + 2 * pairs:2], lengths[2:2 + 2 * pairs:2]
    slack = jnp.minimum(source_of - 1, limit - taker)
    moved = jax.random.randint(jax.random.fold_in(stream_key, 1), (pairs,), 0, 1 << 20) % (slack + 1)
    lengths = lengths.at[1:1 + 2 * pairs:2].set(source_of - moved).at[2:2 + 2 * pairs:2].set(taker + moved)
    return lengths[jax.random.permutation(jax.random.fold_in(stream_key, 2), count)]


def gaussian(rng, dims, scale, reach, split=(), held_as=jnp.bfloat16):
    values = jax.random.normal(rng, dims, jnp.float32) * scale
    if len(split) > 0:
        values = block_scale(rng, dims, split, -0.22, 0.18) * values
    return jnp.clip(values, min=-reach, max=reach).astype(held_as)


def setup_inputs(seed: int = 0, part: int = 0) -> dict:
    key_of = jax.random.split(jax.random.key(seed), 5)
    part_splits = jax.random.split(jax.random.fold_in(key_of[4], part), 5)
    return {
        "queries": draw_queries(jax.random.fold_in(jax.random.fold_in(key_of[4], part), 71), part),
        "keys": draw_keys(jax.random.fold_in(jax.random.fold_in(key_of[4], part), 71), part),
        "values": gaussian(part_splits[2], (SEQ, HEADS * HEAD_DIM), 1.0, 6.0, ((0, 4), (1, 4))),
        "step_of": jnp.searchsorted(jnp.cumsum(ragged_sizes(part_splits[3], STEPS, SEQ, MOST, 1)), jnp.arange(SEQ), side="right").astype(jnp.int32),
    }


def head_rows(q_rows, q_steps, keys_head, values_head, step_of):
    scores = jnp.dot(q_rows, keys_head.T, preferred_element_type=jnp.float32) * (1.0 / math.sqrt(HEAD_DIM))
    visible = step_of[None, :] <= q_steps[:, None]
    row_max = lax.optimization_barrier(jnp.max(jnp.where(visible, scores, -jnp.inf), axis=1, keepdims=True))
    weights = jnp.where(visible, jnp.exp(scores - row_max), 0.0)
    total = lax.optimization_barrier(jnp.sum(weights, axis=1, keepdims=True))
    mixed = jnp.dot(weights.astype(jnp.bfloat16), values_head, preferred_element_type=jnp.float32)
    return (mixed / total).astype(jnp.bfloat16)

def reference(queries, keys, values, step_of):
    block_rows = min(256, SEQ)
    block_count = SEQ // block_rows
    keys_heads = jnp.transpose(keys.reshape(SEQ, HEADS, HEAD_DIM), (1, 0, 2))
    values_heads = jnp.transpose(values.reshape(SEQ, HEADS, HEAD_DIM), (1, 0, 2))

    def one_block(index):
        start = (index * block_rows).astype(jnp.int32)
        q_rows = lax.dynamic_slice_in_dim(queries, start, block_rows, 0)
        q_steps = lax.dynamic_slice_in_dim(step_of, start, block_rows, 0)
        q_heads = jnp.transpose(q_rows.reshape(block_rows, HEADS, HEAD_DIM), (1, 0, 2))

        def one_head(head):
            return head_rows(q_heads[head], q_steps, keys_heads[head], values_heads[head], step_of)
        outputs = lax.map(one_head, jnp.arange(HEADS, dtype=jnp.int32))
        return jnp.transpose(outputs, (1, 0, 2)).reshape(block_rows, HEADS * HEAD_DIM)
    blocks = lax.map(one_block, jnp.arange(block_count, dtype=jnp.int32))
    return blocks.reshape(SEQ, HEADS * HEAD_DIM)
```

```python
import functools
import math

import jax
import jax.numpy as jnp
from jax import lax
from jax.experimental import pallas as pl
from jax.experimental.pallas import tpu as pltpu
from jax.sharding import PartitionSpec as P

HEAD_DIM = 128
LANES = 128
LOW_SCORE = -1e30
UNSEEN = -float(1 << 20)
CHUNKS = (2, 2)
GROUPS = (1, 1)
ANY = pl.BlockSpec(memory_space=pl.ANY)


def attend_half(q_rows, q_steps, keys_all, values_all, key_steps, block_keys):
    row_count, width = q_rows.shape
    head_size = HEAD_DIM
    head_count = width // head_size
    key_count = keys_all.shape[0]
    block_count = key_count // block_keys
    factor_scale = 1.0 / math.sqrt(head_size)
    q_heads = q_rows.reshape(row_count, head_count, head_size)
    blocks = (
        keys_all.reshape(block_count, block_keys, head_count, head_size),
        values_all.reshape(block_count, block_keys, head_count, head_size),
        key_steps.reshape(block_count, block_keys),
    )
    last_step = q_steps[row_count - 1]

    def compute(carry, key_block, value_block, step_block):
        run_max, run_sum, run_out = carry
        scores = (
            jnp.einsum("rhd,khd->hkr", q_heads, key_block, preferred_element_type=jnp.float32)
            * factor_scale
        )
        visible = step_block[None, :, None] <= q_steps[None, None, :]
        masked = jnp.where(visible, scores, LOW_SCORE)
        new_max = jnp.maximum(run_max, jnp.max(masked, axis=1))
        weights = jnp.where(visible, jnp.exp(masked - new_max[:, None, :]), 0.0)
        rescale = jnp.exp(run_max - new_max)
        new_sum = run_sum * rescale + jnp.sum(weights, axis=1)
        update = jnp.einsum(
            "hkr,khd->rhd",
            weights.astype(jnp.bfloat16),
            value_block,
            preferred_element_type=jnp.float32,
        )
        new_out = run_out * jnp.transpose(rescale)[:, :, None] + update
        return (new_max, new_sum, new_out)

    def visit(carry, block):
        key_block, value_block, step_block = block
        result = lax.cond(
            step_block[0] <= last_step,
            lambda state: compute(state, key_block, value_block, step_block),
            lambda state: state,
            carry,
        )
        return (result, None)

    initial = (
        jnp.full((head_count, row_count), LOW_SCORE, jnp.float32),
        jnp.zeros((head_count, row_count), jnp.float32),
        jnp.zeros((row_count, head_count, head_size), jnp.float32),
    )
    final_state, unused = lax.scan(visit, initial, blocks)
    return final_state


def on_any(queries, keys, values, step_of):
    block_rows, width = queries.shape
    head_size = HEAD_DIM
    head_count = width // head_size
    key_parts = lax.axis_size("ka")
    query_index = lax.axis_index("pb")
    key_index = lax.axis_index("ka")
    shard_rows = block_rows // key_parts
    half_rows = block_rows // 2
    key_count = keys.shape[0]
    first_steps = lax.dynamic_slice_in_dim(step_of, query_index * block_rows, half_rows)
    second_steps = lax.dynamic_slice_in_dim(
        step_of, query_index * block_rows + half_rows, half_rows
    )
    keys_mine, values_mine = (keys, values)
    key_steps = lax.dynamic_slice_in_dim(step_of, key_index * key_count, key_count)
    keys_all, values_all = (
        lax.all_gather(keys_mine, "pb", axis=1, tiled=True),
        lax.all_gather(values_mine, "pb", axis=1, tiled=True),
    )
    block_keys = math.gcd(64, key_count)
    first_state = attend_half(
        queries[:half_rows], first_steps, keys_all, values_all, key_steps, block_keys
    )
    second_state = attend_half(
        queries[half_rows:], second_steps, keys_all, values_all, key_steps, block_keys
    )
    row_max = jnp.concatenate([first_state[0], second_state[0]], axis=1)
    row_sum = jnp.concatenate([first_state[1], second_state[1]], axis=1)
    row_out = jnp.concatenate([first_state[2], second_state[2]], axis=0)
    sent = (
        jnp.transpose(row_max)[:, None, :],
        jnp.transpose(row_sum)[:, None, :],
        row_out.reshape(block_rows, 1, width),
    )
    got_max, got_sum, got_out = (
        lax.all_to_all(sent[0], "ka", split_axis=0, concat_axis=1, tiled=True),
        lax.all_to_all(sent[1], "ka", split_axis=0, concat_axis=1, tiled=True),
        lax.all_to_all(sent[2], "ka", split_axis=0, concat_axis=1, tiled=True),
    )
    best = jnp.max(got_max, axis=1, keepdims=True)
    weight = jnp.exp(got_max - best)
    total = jnp.sum(got_sum * weight, axis=1)
    shares = weight / total[:, None, :]
    pieces = got_out.reshape(shard_rows, key_parts, head_count, head_size) * shares[:, :, :, None]
    result = jnp.sum(pieces, axis=1).reshape(shard_rows, width)
    result = result.astype(jnp.bfloat16)
    return result

def attend_kernel(heads, first, q_first, scale, steps_ref, queries, q_1, q_2, q_3, keys, values, got,
                  own, up, down, far, q_buf, k_buf, v_buf, stats_buf, parts, sem, out_sem):
    column = lax.axis_index("pb")
    z = lax.axis_index("ka")
    rows = queries.shape[0]
    half_rows = rows // 2
    sub = rows // 4
    width = heads * HEAD_DIM
    held = keys.shape[0]
    pair = 2 * held
    upper, half = z // 2, z % 2

    def place(block):
        return (block + 4 - 2 * upper) % 4

    mine = pl.multiple_of(half * held, held)
    other = pl.multiple_of((1 - half) * held, held)
    base = pl.multiple_of(column * keys.shape[1] + first * HEAD_DIM, HEAD_DIM)
    at = pl.ds(first * HEAD_DIM, width)
    q_at = pl.ds(q_first * HEAD_DIM, width)
    copies = [
        (keys.at[:, at], k_buf.at[pl.ds(mine, held), :]),
        (got.at[0], k_buf.at[pl.ds(other, held), :]),
        (queries.at[pl.ds(pl.multiple_of(half * half_rows, half_rows), half_rows), pl.ds(base, width)], q_buf.at[place(column)]),
    ]
    copies += [(q.at[:, q_at], q_buf.at[place(column ^ d)]) for d, q in ((1, q_1), (2, q_2), (3, q_3))]
    for h in range(heads):
        to = pl.ds(2 * h * HEAD_DIM, HEAD_DIM)
        copies += [
            (values.at[:, pl.ds((first + h) * HEAD_DIM, HEAD_DIM)], v_buf.at[pl.ds(mine, held), to]),
            (got.at[1, :, pl.ds(h * HEAD_DIM, HEAD_DIM)], v_buf.at[pl.ds(other, held), to]),
        ]
    copies = [pltpu.make_async_copy(a, b, sem.at[i]) for i, (a, b) in enumerate(copies)]
    for copy in copies:
        copy.start()
    for h in range(heads):
        v_buf[:, (2 * h + 1) * HEAD_DIM:(2 * h + 2) * HEAD_DIM] = jnp.ones((pair, HEAD_DIM), jnp.bfloat16)
    stats_buf[...] = jnp.zeros(stats_buf.shape, jnp.float32)
    columns = jnp.transpose(steps_ref[...].astype(jnp.float32))
    group = lax.broadcasted_iota(jnp.int32, columns.shape, 1)
    tiles = pair // LANES
    key_steps = steps_ref[pl.ds(pl.multiple_of(upper * tiles, tiles), tiles), :].astype(jnp.float32)
    for copy in copies:
        copy.wait()

    def tile(slot, limit, masked_from, start=0, count=half_rows):
        q = q_buf[slot, start:start + count, :]
        block = (slot + 2 * upper) % 4
        if masked_from < limit:
            q_steps = jnp.concatenate([
                jnp.sum(jnp.where(group == block * 4 + half * 2 + j, columns, 0.0), axis=1, keepdims=True)
                for j in range(start // sub, (start + count) // sub)
            ], axis=0)
            k_steps = jnp.concatenate([key_steps[j:j + 1] for j in range(masked_from // LANES, limit // LANES)], axis=1)
            visible = k_steps <= q_steps
        lane = lax.broadcasted_iota(jnp.int32, (count, LANES), 1)
        stats = stats_buf[start:start + count, :]
        for h in range(heads):
            cut = slice(h * HEAD_DIM, (h + 1) * HEAD_DIM)
            scores = lax.dot_general(q[:, cut], k_buf[:limit, cut], (((1,), (1,)), ((), ())),
                                     preferred_element_type=jnp.float32)
            if masked_from < limit:
                seen = jnp.where(visible, scores[:, masked_from:], UNSEEN / scale)
                scores = seen if masked_from == 0 else jnp.concatenate([scores[:, :masked_from], seen], axis=1)
            top = jnp.max(scores, axis=1, keepdims=True) * scale
            top = top.astype(jnp.bfloat16).astype(jnp.float32)
            weights = jnp.exp2(scores * scale - top).astype(jnp.bfloat16)
            mixed = lax.dot_general(weights, v_buf[:limit, 2 * h * HEAD_DIM:(2 * h + 2) * HEAD_DIM],
                                    (((1,), (0,)), ((), ())), preferred_element_type=jnp.float32)
            total = mixed[:, HEAD_DIM:]
            index = slot * heads + h
            result = (mixed[:, :HEAD_DIM] / total).astype(jnp.bfloat16)
            for j in range(count // sub):
                parts[start // sub + j, 1 + index] = result[j * sub:(j + 1) * sub]
            high = total.astype(jnp.bfloat16).astype(jnp.float32)
            stats = jnp.where(lane == 3 * index, top, stats)
            stats = jnp.where(lane == 3 * index + 1, high, stats)
            stats = jnp.where(lane == 3 * index + 2, total - high, stats)
        stats_buf[start:start + count, :] = stats

    for which in (0, 1):
        @pl.when(half == which)
        def _():
            reach = held // 2 + LANES if which == 0 else held + LANES
            tile(0, reach, 0)
            tile(1, min(held + reach, pair), held)

    @pl.when(upper == 0)
    def _():
        tile(2, pair, pair)
        tile(3, pair, pair)

    @pl.when(z == 3)
    def _():
        tile(3, LANES, 0, start=sub, count=sub)

    for j in range(2):
        parts[j, 0] = stats_buf[j * sub:(j + 1) * sub, :].astype(jnp.bfloat16)
    for which, pair_of in enumerate(((own, up), (up, far), (far, down), (down, own))):
        @pl.when(z == which)
        def _():
            out = [pltpu.make_async_copy(parts.at[j, pl.ds(0, to.shape[0])], to, out_sem.at[j]) for j, to in enumerate(pair_of)]
            for copy in out:
                copy.start()
            for copy in out:
                copy.wait()


def attend(heads, first, q_first, steps, queries, moved, keys, values, got):
    rows = queries.shape[0]
    held = keys.shape[0]
    sub = rows // 4
    part = jax.ShapeDtypeStruct((4 * heads + 1, sub, LANES), jnp.bfloat16)
    short = jax.ShapeDtypeStruct((2 * heads + 1, sub, LANES), jnp.bfloat16)
    exps = heads * 4 * (rows // 2) * held * 2
    return pl.pallas_call(
        functools.partial(attend_kernel, heads, first, q_first, math.log2(math.e) / math.sqrt(HEAD_DIM)),
        out_shape=[part, part, short, part],
        in_specs=[pl.BlockSpec(memory_space=pltpu.VMEM)] + [ANY] * 7,
        out_specs=[ANY] * 4,
        scratch_shapes=[
            pltpu.VMEM((4, rows // 2, heads * HEAD_DIM), jnp.bfloat16),
            pltpu.VMEM((2 * held, heads * HEAD_DIM), jnp.bfloat16),
            pltpu.VMEM((2 * held, 2 * heads * HEAD_DIM), jnp.bfloat16),
            pltpu.VMEM((rows // 2, LANES), jnp.float32),
            pltpu.VMEM((2,) + part.shape, jnp.bfloat16),
            pltpu.SemaphoreType.DMA((6 + 2 * heads,)),
            pltpu.SemaphoreType.DMA((2,)),
        ],
        compiler_params=pltpu.CompilerParams(vmem_limit_bytes=40 << 20),
        cost_estimate=pl.CostEstimate(flops=exps * 4 * HEAD_DIM, bytes_accessed=4 << 20, transcendentals=exps),
        name="attend",
    )(steps, queries, *moved, keys, values, got)


def merge_kernel(chunks, *refs):
    count = len(chunks)
    ins, outs, (low, high, result, sem) = refs[:4 * count], refs[4 * count:4 * count + 4], refs[4 * count + 4:]
    column = lax.axis_index("pb")
    z = lax.axis_index("ka")
    starts = [sum(4 * heads + 1 for heads in chunks[:c]) for c in range(count)]
    for which in range(4):
        @pl.when(z == which)
        def _():
            copies = []
            for c, heads in enumerate(chunks):
                own, up, down, far = ins[4 * c:4 * c + 4]
                for held, sent in zip((low, high), ((own, far), (up, down), (up, down), (far, own))[which]):
                    at = pl.ds(starts[c], sent.shape[0])
                    copies.append(pltpu.make_async_copy(sent, held.at[at], sem.at[len(copies)]))
            for copy in copies:
                copy.start()
            for copy in copies:
                copy.wait()

    def merge_block(block):
        first = 0
        for c, heads in enumerate(chunks):
            stats = [held[starts[c]].astype(jnp.float32) for held in (low, high)]
            for h in range(heads):
                places = [slot * heads + h for slot in (block, (block + 2) % 4)]
                cut = slice((first + h) * HEAD_DIM, (first + h + 1) * HEAD_DIM)
                tops = [s[:, 3 * i:3 * i + 1] for s, i in zip(stats, places)]
                totals = [s[:, 3 * i + 1:3 * i + 2] + s[:, 3 * i + 2:3 * i + 3] for s, i in zip(stats, places)]
                best = jnp.maximum(*tops)
                shares = [total * jnp.exp2(top - best) for top, total in zip(tops, totals)]
                share = shares[0] / (shares[0] + shares[1])
                a = low[starts[c] + 1 + places[0]].astype(jnp.float32)
                b = high[starts[c] + 1 + places[1]].astype(jnp.float32)
                result[block, :, cut] = (a * share + b * (1.0 - share)).astype(jnp.bfloat16)
            first += heads

    def take_block(block):
        first = 0
        for c, heads in enumerate(chunks):
            for h in range(heads):
                cut = slice((first + h) * HEAD_DIM, (first + h + 1) * HEAD_DIM)
                result[block, :, cut] = low[starts[c] + 1 + block * heads + h]
            first += heads

    take_block(0)

    @pl.when(z < 3)
    def _():
        take_block(1)

    @pl.when(z == 3)
    def _():
        merge_block(1)

    merge_block(2)
    merge_block(3)
    copies = [pltpu.make_async_copy(result.at[column ^ d], out, sem.at[d]) for d, out in enumerate(outs)]
    for copy in copies:
        copy.start()
    for copy in copies:
        copy.wait()


def merge(chunks, parts):
    sub = parts[0].shape[1]
    tiles = sum(4 * heads + 1 for heads in chunks)
    block = jax.ShapeDtypeStruct((sub, sum(chunks) * HEAD_DIM), jnp.bfloat16)
    return pl.pallas_call(
        functools.partial(merge_kernel, chunks),
        out_shape=[block] * 4,
        in_specs=[ANY] * len(parts),
        out_specs=[ANY] * 4,
        scratch_shapes=[
            pltpu.VMEM((tiles, sub, LANES), jnp.bfloat16),
            pltpu.VMEM((tiles, sub, LANES), jnp.bfloat16),
            pltpu.VMEM((4,) + block.shape, jnp.bfloat16),
            pltpu.SemaphoreType.DMA((max(4, 2 * len(chunks)),)),
        ],
        compiler_params=pltpu.CompilerParams(vmem_limit_bytes=16 << 20),
        cost_estimate=pl.CostEstimate(flops=1 << 20, bytes_accessed=4 << 20, transcendentals=0),
        name="merge",
    )(*parts)


def assemble_kernel(widths, *refs):
    column = lax.axis_index("pb")
    pieces, out = refs[:-1], refs[-1]
    first = 0
    for g, width in enumerate(widths):
        for d in range(4):
            at = pl.multiple_of((column ^ d) * sum(widths) + first, HEAD_DIM)
            out[:, pl.ds(at, width)] = pieces[4 * g + d][...]
        first += width


def assemble(pieces):
    sub = pieces[0].shape[0]
    widths = [piece.shape[1] for piece in pieces[::4]]
    return pl.pallas_call(
        functools.partial(assemble_kernel, widths),
        out_shape=jax.ShapeDtypeStruct((sub, 4 * sum(widths)), jnp.bfloat16),
        in_specs=[pl.BlockSpec(memory_space=pltpu.VMEM)] * len(pieces),
        out_specs=pl.BlockSpec(memory_space=pltpu.VMEM),
        name="assemble",
    )(*pieces)


def on_line(queries, keys, values, step_of):
    column = lax.axis_index("pb")
    half = lax.axis_index("ka") % 2
    half_rows = queries.shape[0] // 2
    block = keys.shape[1]
    steps = step_of.reshape(-1, LANES)
    swaps = [[(i, i ^ d) for i in range(4)] for d in (1, 2, 3)]
    ready = []
    first = 0
    chunk = 0
    for size in GROUPS:
        group = CHUNKS[chunk:chunk + size]
        start = first
        width = sum(group) * HEAD_DIM
        moved = []
        for heads in group:
            at = slice(first * HEAD_DIM, (first + heads) * HEAD_DIM)
            got = lax.ppermute(jnp.stack([keys[:, at], values[:, at]]), "ka", [(0, 1), (1, 0), (2, 3), (3, 2)])
            if not moved:
                for d in (1, 2, 3):
                    corner = (half * half_rows, (column ^ d) * block + start * HEAD_DIM)
                    sent = lax.dynamic_slice(queries, corner, (half_rows, width))
                    moved.append(lax.ppermute(sent, "pb", swaps[d - 1]))
            ready.append((heads, first, first - start, got, moved))
            first += heads
        chunk += size
    pieces = []
    chunk = 0
    for size in GROUPS:
        parts = []
        for heads, first, q_first, got, moved in ready[chunk:chunk + size]:
            own, up, down, far = attend(heads, first, q_first, steps, queries, moved, keys, values, got)
            parts += [
                own,
                lax.ppermute(up, "ka", [(0, 1), (1, 2)]),
                lax.ppermute(down, "ka", [(3, 2), (2, 1)]),
                lax.ppermute(far, "ka", [(1, 3), (2, 0)]),
            ]
        sent = merge(CHUNKS[chunk:chunk + size], parts)
        pieces += [sent[0]] + [lax.ppermute(sent[d], "pb", swaps[d - 1]) for d in (1, 2, 3)]
        chunk += size
    return assemble(pieces)


def on_device(queries, keys, values, step_of):
    rows, width = queries.shape
    held, block = keys.shape
    line = (
        lax.axis_size("pb") == 4
        and lax.axis_size("ka") == 4
        and held == rows == 4 * LANES
        and block == sum(CHUNKS) * HEAD_DIM
    )
    if line:
        return on_line(queries, keys, values, step_of)
    return on_any(queries, keys, values, step_of)


def solution(mesh):
    placed = (
        P(("groups", "pb"), None),
        P(("groups", "ka"), "pb"),
        P(("groups", "ka"), "pb"),
        P("groups"),
    )
    return jax.shard_map(
        on_device,
        mesh=mesh,
        in_specs=placed,
        out_specs=P(("groups", "pb", "ka"), None),
        check_vma=False,
    )
```

```python
import functools
import math

import jax
import jax.numpy as jnp
from jax import lax
from jax.experimental import pallas as pl
from jax.experimental.pallas import tpu as pltpu
from jax.sharding import PartitionSpec as P

HEAD_DIM = 128
LANES = 128
LOW_SCORE = -1e30
ROW_TILE = 256
ANY = pl.BlockSpec(memory_space=pl.ANY)


def attend_half(q_rows, q_steps, keys_all, values_all, key_steps, block_keys):
    row_count, width = q_rows.shape
    head_size = HEAD_DIM
    head_count = width // head_size
    key_count = keys_all.shape[0]
    block_count = key_count // block_keys
    factor_scale = 1.0 / math.sqrt(head_size)
    q_heads = q_rows.reshape(row_count, head_count, head_size)
    blocks = (
        keys_all.reshape(block_count, block_keys, head_count, head_size),
        values_all.reshape(block_count, block_keys, head_count, head_size),
        key_steps.reshape(block_count, block_keys),
    )
    last_step = q_steps[row_count - 1]

    def compute(carry, key_block, value_block, step_block):
        run_max, run_sum, run_out = carry
        scores = (
            jnp.einsum("rhd,khd->hkr", q_heads, key_block, preferred_element_type=jnp.float32)
            * factor_scale
        )
        visible = step_block[None, :, None] <= q_steps[None, None, :]
        masked = jnp.where(visible, scores, LOW_SCORE)
        new_max = jnp.maximum(run_max, jnp.max(masked, axis=1))
        weights = jnp.where(visible, jnp.exp(masked - new_max[:, None, :]), 0.0)
        rescale = jnp.exp(run_max - new_max)
        new_sum = run_sum * rescale + jnp.sum(weights, axis=1)
        update = jnp.einsum(
            "hkr,khd->rhd",
            weights.astype(jnp.bfloat16),
            value_block,
            preferred_element_type=jnp.float32,
        )
        new_out = run_out * jnp.transpose(rescale)[:, :, None] + update
        return (new_max, new_sum, new_out)

    def visit(carry, block):
        key_block, value_block, step_block = block
        result = lax.cond(
            step_block[0] <= last_step,
            lambda state: compute(state, key_block, value_block, step_block),
            lambda state: state,
            carry,
        )
        return (result, None)

    initial = (
        jnp.full((head_count, row_count), LOW_SCORE, jnp.float32),
        jnp.zeros((head_count, row_count), jnp.float32),
        jnp.zeros((row_count, head_count, head_size), jnp.float32),
    )
    final_state, unused = lax.scan(visit, initial, blocks)
    return final_state


def on_any(queries, keys, values, step_of):
    block_rows, width = queries.shape
    head_size = HEAD_DIM
    head_count = width // head_size
    key_parts = lax.axis_size("ka")
    query_index = lax.axis_index("pb")
    key_index = lax.axis_index("ka")
    shard_rows = block_rows // key_parts
    half_rows = block_rows // 2
    key_count = keys.shape[0]
    first_steps = lax.dynamic_slice_in_dim(step_of, query_index * block_rows, half_rows)
    second_steps = lax.dynamic_slice_in_dim(
        step_of, query_index * block_rows + half_rows, half_rows
    )
    keys_mine, values_mine = (keys, values)
    key_steps = lax.dynamic_slice_in_dim(step_of, key_index * key_count, key_count)
    keys_all, values_all = (
        lax.all_gather(keys_mine, "pb", axis=1, tiled=True),
        lax.all_gather(values_mine, "pb", axis=1, tiled=True),
    )
    block_keys = math.gcd(64, key_count)
    first_state = attend_half(
        queries[:half_rows], first_steps, keys_all, values_all, key_steps, block_keys
    )
    second_state = attend_half(
        queries[half_rows:], second_steps, keys_all, values_all, key_steps, block_keys
    )
    row_max = jnp.concatenate([first_state[0], second_state[0]], axis=1)
    row_sum = jnp.concatenate([first_state[1], second_state[1]], axis=1)
    row_out = jnp.concatenate([first_state[2], second_state[2]], axis=0)
    sent = (
        jnp.transpose(row_max)[:, None, :],
        jnp.transpose(row_sum)[:, None, :],
        row_out.reshape(block_rows, 1, width),
    )
    got_max, got_sum, got_out = (
        lax.all_to_all(sent[0], "ka", split_axis=0, concat_axis=1, tiled=True),
        lax.all_to_all(sent[1], "ka", split_axis=0, concat_axis=1, tiled=True),
        lax.all_to_all(sent[2], "ka", split_axis=0, concat_axis=1, tiled=True),
    )
    best = jnp.max(got_max, axis=1, keepdims=True)
    weight = jnp.exp(got_max - best)
    total = jnp.sum(got_sum * weight, axis=1)
    shares = weight / total[:, None, :]
    pieces = got_out.reshape(shard_rows, key_parts, head_count, head_size) * shares[:, :, :, None]
    result = jnp.sum(pieces, axis=1).reshape(shard_rows, width)
    result = result.astype(jnp.bfloat16)
    return result

def pack_kernel(queries, keys, values, *refs):
    outs, sem = refs[:6], refs[6]
    column = lax.axis_index("pb")
    z = lax.axis_index("ka")
    copies = []
    for d, out in zip((1, 2, 3), outs[:3]):
        head = pl.ds(pl.multiple_of((z ^ d) * HEAD_DIM, HEAD_DIM), HEAD_DIM)
        copies += [(keys.at[:, head], out.at[0]), (values.at[:, head], out.at[1])]
    for d, out in zip((1, 2, 3), outs[3:]):
        head = pl.ds(pl.multiple_of((column ^ d) * keys.shape[1] + z * HEAD_DIM, HEAD_DIM), HEAD_DIM)
        copies.append((queries.at[:, head], out))
    copies = [pltpu.make_async_copy(a, b, sem.at[i]) for i, (a, b) in enumerate(copies)]
    for copy in copies:
        copy.start()
    for copy in copies:
        copy.wait()


def pack(queries, keys, values):
    pair = jax.ShapeDtypeStruct((2, keys.shape[0], HEAD_DIM), keys.dtype)
    head = jax.ShapeDtypeStruct((queries.shape[0], HEAD_DIM), queries.dtype)
    return pl.pallas_call(
        pack_kernel,
        out_shape=[pair] * 3 + [head] * 3,
        in_specs=[ANY] * 3,
        out_specs=[pl.BlockSpec(memory_space=pltpu.VMEM)] * 6,
        scratch_shapes=[pltpu.SemaphoreType.DMA((9,))],
        name="pack",
    )(queries, keys, values)


def split_keys(start, length, late, held):
    limit = min(start + ROW_TILE + LANES, length)
    low, high = min(late * held, limit), min((late + 1) * held, limit)
    early = [cut for cut in ((0, low), (high, limit)) if cut[0] < cut[1]]
    return early, [(low, high)] if low < high else []


def scores_of(q, start, cuts, base, k_buf, steps, columns):
    q_steps = jnp.concatenate([columns[:, g:g + 1] for g in range(start // LANES, (start + ROW_TILE) // LANES)], axis=0)
    found = []
    for low, high in cuts:
        scores = lax.dot_general(q, k_buf[low - base:high - base, :], (((1,), (1,)), ((), ())),
                                 preferred_element_type=jnp.float32)
        first = max(low, start)
        if first < high:
            k_steps = jnp.concatenate([steps[g:g + 1] for g in range(first // LANES, high // LANES)], axis=1)
            seen = jnp.where(k_steps <= q_steps, scores[:, first - low:], LOW_SCORE)
            scores = jnp.concatenate([scores[:, :first - low], seen], axis=1) if low < first else seen
        found.append(scores)
    return jnp.concatenate(found, axis=1) if len(found) > 1 else found[0]


def weigh(weights, cuts, base, v_buf):
    mixed = None
    at = 0
    for low, high in cuts:
        part = lax.dot_general(weights[:, at:at + high - low], v_buf[low - base:high - base, :], (((1,), (0,)), ((), ())),
                               preferred_element_type=jnp.float32)
        mixed = part if mixed is None else mixed + part
        at += high - low
    return mixed


def early_kernel(scale, steps_ref, queries, q_1, q_2, q_3, keys, values, got_1, got_2, sums, stats, q_buf, k_buf, v_buf, sem):
    column = lax.axis_index("pb")
    z = lax.axis_index("ka")
    rows = queries.shape[0]
    held = keys.shape[0]
    length = k_buf.shape[0]
    head = pl.ds(pl.multiple_of(z * HEAD_DIM, HEAD_DIM), HEAD_DIM)
    query_head = pl.ds(pl.multiple_of(column * keys.shape[1] + z * HEAD_DIM, HEAD_DIM), HEAD_DIM)
    left = pl.ds(0, HEAD_DIM)

    def block(index, size):
        return pl.ds(pl.multiple_of(index * size, size), size)

    copies = [
        (queries.at[:, query_head], q_buf.at[block(column, rows), :]),
        (keys.at[:, head], k_buf.at[block(z, held), :]),
        (values.at[:, head], v_buf.at[block(z, held), left]),
    ]
    copies += [(q, q_buf.at[block(column ^ d, rows), :]) for d, q in ((1, q_1), (2, q_2), (3, q_3))]
    for d, got in ((1, got_1), (2, got_2)):
        copies += [
            (got.at[0], k_buf.at[block(z ^ d, held), :]),
            (got.at[1], v_buf.at[block(z ^ d, held), left]),
        ]
    copies = [pltpu.make_async_copy(a, b, sem.at[i]) for i, (a, b) in enumerate(copies)]
    for copy in copies:
        copy.start()
    v_buf[:, HEAD_DIM:] = jnp.ones((length, HEAD_DIM), jnp.bfloat16)
    steps = steps_ref[...].astype(jnp.float32)
    columns = jnp.transpose(steps)
    lane = lax.broadcasted_iota(jnp.int32, (ROW_TILE, LANES), 1)
    for copy in copies:
        copy.wait()
    for which in range(4):
        @pl.when(z == which)
        def _():
            for start in range(0, length, ROW_TILE):
                tile = slice(start, start + ROW_TILE)
                cuts, _ = split_keys(start, length, which ^ 3, held)
                if not cuts:
                    continue
                scores = scores_of(q_buf[tile, :], start, cuts, 0, k_buf, steps, columns)
                top = jnp.max(scores, axis=1, keepdims=True) * scale
                mixed = weigh(jnp.exp2(scores * scale - top).astype(jnp.bfloat16), cuts, 0, v_buf)
                sums[tile, :] = mixed[:, :HEAD_DIM]
                stats[tile, :] = jnp.where(lane < LANES // 2, top, mixed[:, HEAD_DIM:])


def late_kernel(scale, steps_ref, q_buf, sums, stats, got, out, v_buf):
    z = lax.axis_index("ka")
    held = got.shape[1]
    length = q_buf.shape[0]
    v_buf[:, :HEAD_DIM] = got[1]
    v_buf[:, HEAD_DIM:] = jnp.ones((held, HEAD_DIM), jnp.bfloat16)
    steps = steps_ref[...].astype(jnp.float32)
    columns = jnp.transpose(steps)
    k_buf = got.at[0]
    for which in range(4):
        @pl.when(z == which)
        def _():
            late = which ^ 3
            for start in range(0, length, ROW_TILE):
                tile = slice(start, start + ROW_TILE)
                early, cuts = split_keys(start, length, late, held)
                if early:
                    mixed = sums[tile, :]
                    top, total = stats[tile, 0:1], stats[tile, LANES // 2:LANES // 2 + 1]
                if cuts:
                    scores = scores_of(q_buf[tile, :], start, cuts, late * held, k_buf, steps, columns)
                    best = jnp.max(scores, axis=1, keepdims=True) * scale
                    if early:
                        best = jnp.maximum(best, top)
                    added = weigh(jnp.exp2(scores * scale - best).astype(jnp.bfloat16), cuts, late * held, v_buf)
                    if early:
                        kept = jnp.exp2(top - best)
                        mixed = mixed * kept + added[:, :HEAD_DIM]
                        total = total * kept + added[:, HEAD_DIM:]
                    else:
                        mixed, total = added[:, :HEAD_DIM], added[:, HEAD_DIM:]
                out[tile, :] = (mixed / total).astype(jnp.bfloat16)


def attend(steps, queries, moved, keys, values, got):
    length = steps.shape[0] * LANES
    held = keys.shape[0]
    exps = length * (length // 2 + LANES)
    scale = math.log2(math.e) / math.sqrt(HEAD_DIM)
    vmem = pl.BlockSpec(memory_space=pltpu.VMEM)
    head = jax.ShapeDtypeStruct((length, HEAD_DIM), jnp.bfloat16)
    held_sums = jax.ShapeDtypeStruct((length, HEAD_DIM), jnp.float32)
    sums, stats, gathered = pl.pallas_call(
        functools.partial(early_kernel, scale),
        out_shape=[held_sums, held_sums, head],
        in_specs=[vmem] + [ANY] * 8,
        out_specs=[vmem] * 3,
        scratch_shapes=[
            pltpu.VMEM((length, HEAD_DIM), jnp.bfloat16),
            pltpu.VMEM((length, 2 * HEAD_DIM), jnp.bfloat16),
            pltpu.SemaphoreType.DMA((10,)),
        ],
        compiler_params=pltpu.CompilerParams(vmem_limit_bytes=40 << 20),
        cost_estimate=pl.CostEstimate(flops=exps * 4 * HEAD_DIM, bytes_accessed=4 << 20, transcendentals=exps),
        name="attend_early",
    )(steps, queries, *moved, keys, values, *got[:2])
    return pl.pallas_call(
        functools.partial(late_kernel, scale),
        out_shape=head,
        in_specs=[vmem] * 5,
        out_specs=vmem,
        scratch_shapes=[pltpu.VMEM((held, 2 * HEAD_DIM), jnp.bfloat16)],
        compiler_params=pltpu.CompilerParams(vmem_limit_bytes=40 << 20),
        cost_estimate=pl.CostEstimate(flops=exps * HEAD_DIM, bytes_accessed=4 << 20, transcendentals=exps // 4),
        name="attend_late",
    )(steps, gathered, sums, stats, got[2])


def one_head_each(queries, keys, values, step_of):
    swaps = [[(i, i ^ d) for i in range(4)] for d in (1, 2, 3)]
    packed = pack(queries, keys, values)
    got = [lax.ppermute(piece, "ka", swap) for piece, swap in zip(packed[:3], swaps)]
    moved = [lax.ppermute(piece, "pb", swap) for piece, swap in zip(packed[3:], swaps)]
    done = attend(step_of.reshape(-1, LANES), queries, moved, keys, values, got)
    rows = done.shape[0] // 16
    pieces = lax.all_to_all(done.reshape(16, rows, HEAD_DIM), ("pb", "ka"), split_axis=0, concat_axis=0, tiled=True)
    return jnp.transpose(pieces, (1, 0, 2)).reshape(rows, 16 * HEAD_DIM)


def on_device(queries, keys, values, step_of):
    rows = queries.shape[0]
    held, block = keys.shape
    square = (
        lax.axis_size("pb") == 4
        and lax.axis_size("ka") == 4
        and held == rows == 4 * LANES
        and block == 4 * HEAD_DIM
    )
    if square:
        return one_head_each(queries, keys, values, step_of)
    return on_any(queries, keys, values, step_of)


def solution(mesh):
    placed = (
        P(("groups", "pb"), None),
        P(("groups", "ka"), "pb"),
        P(("groups", "ka"), "pb"),
        P("groups"),
    )
    return jax.shard_map(
        on_device,
        mesh=mesh,
        in_specs=placed,
        out_specs=P(("groups", "pb", "ka"), None),
        check_vma=False,
    )
```

```python
import functools
import math

import jax
import jax.numpy as jnp
from jax import lax
from jax.experimental import pallas as pl
from jax.experimental.pallas import tpu as pltpu
from jax.sharding import PartitionSpec as P

HEAD_DIM = 128
LANES = 128
LOW_SCORE = -1e30
UNSEEN = -float(1 << 20)
ROW_TILE = 256
STATS = 16
ANY = pl.BlockSpec(memory_space=pl.ANY)
VMEM = pl.BlockSpec(memory_space=pltpu.VMEM)


def attend_half(q_rows, q_steps, keys_all, values_all, key_steps, block_keys):
    row_count, width = q_rows.shape
    head_size = HEAD_DIM
    head_count = width // head_size
    key_count = keys_all.shape[0]
    block_count = key_count // block_keys
    factor_scale = 1.0 / math.sqrt(head_size)
    q_heads = q_rows.reshape(row_count, head_count, head_size)
    blocks = (
        keys_all.reshape(block_count, block_keys, head_count, head_size),
        values_all.reshape(block_count, block_keys, head_count, head_size),
        key_steps.reshape(block_count, block_keys),
    )
    last_step = q_steps[row_count - 1]

    def compute(carry, key_block, value_block, step_block):
        run_max, run_sum, run_out = carry
        scores = (
            jnp.einsum("rhd,khd->hkr", q_heads, key_block, preferred_element_type=jnp.float32)
            * factor_scale
        )
        visible = step_block[None, :, None] <= q_steps[None, None, :]
        masked = jnp.where(visible, scores, LOW_SCORE)
        new_max = jnp.maximum(run_max, jnp.max(masked, axis=1))
        weights = jnp.where(visible, jnp.exp(masked - new_max[:, None, :]), 0.0)
        rescale = jnp.exp(run_max - new_max)
        new_sum = run_sum * rescale + jnp.sum(weights, axis=1)
        update = jnp.einsum(
            "hkr,khd->rhd",
            weights.astype(jnp.bfloat16),
            value_block,
            preferred_element_type=jnp.float32,
        )
        new_out = run_out * jnp.transpose(rescale)[:, :, None] + update
        return (new_max, new_sum, new_out)

    def visit(carry, block):
        key_block, value_block, step_block = block
        result = lax.cond(
            step_block[0] <= last_step,
            lambda state: compute(state, key_block, value_block, step_block),
            lambda state: state,
            carry,
        )
        return (result, None)

    initial = (
        jnp.full((head_count, row_count), LOW_SCORE, jnp.float32),
        jnp.zeros((head_count, row_count), jnp.float32),
        jnp.zeros((row_count, head_count, head_size), jnp.float32),
    )
    final_state, unused = lax.scan(visit, initial, blocks)
    return final_state


def on_any(queries, keys, values, step_of):
    block_rows, width = queries.shape
    head_size = HEAD_DIM
    head_count = width // head_size
    key_parts = lax.axis_size("ka")
    query_index = lax.axis_index("pb")
    key_index = lax.axis_index("ka")
    shard_rows = block_rows // key_parts
    half_rows = block_rows // 2
    key_count = keys.shape[0]
    first_steps = lax.dynamic_slice_in_dim(step_of, query_index * block_rows, half_rows)
    second_steps = lax.dynamic_slice_in_dim(
        step_of, query_index * block_rows + half_rows, half_rows
    )
    keys_mine, values_mine = (keys, values)
    key_steps = lax.dynamic_slice_in_dim(step_of, key_index * key_count, key_count)
    keys_all, values_all = (
        lax.all_gather(keys_mine, "pb", axis=1, tiled=True),
        lax.all_gather(values_mine, "pb", axis=1, tiled=True),
    )
    block_keys = math.gcd(64, key_count)
    first_state = attend_half(
        queries[:half_rows], first_steps, keys_all, values_all, key_steps, block_keys
    )
    second_state = attend_half(
        queries[half_rows:], second_steps, keys_all, values_all, key_steps, block_keys
    )
    row_max = jnp.concatenate([first_state[0], second_state[0]], axis=1)
    row_sum = jnp.concatenate([first_state[1], second_state[1]], axis=1)
    row_out = jnp.concatenate([first_state[2], second_state[2]], axis=0)
    sent = (
        jnp.transpose(row_max)[:, None, :],
        jnp.transpose(row_sum)[:, None, :],
        row_out.reshape(block_rows, 1, width),
    )
    got_max, got_sum, got_out = (
        lax.all_to_all(sent[0], "ka", split_axis=0, concat_axis=1, tiled=True),
        lax.all_to_all(sent[1], "ka", split_axis=0, concat_axis=1, tiled=True),
        lax.all_to_all(sent[2], "ka", split_axis=0, concat_axis=1, tiled=True),
    )
    best = jnp.max(got_max, axis=1, keepdims=True)
    weight = jnp.exp(got_max - best)
    total = jnp.sum(got_sum * weight, axis=1)
    shares = weight / total[:, None, :]
    pieces = got_out.reshape(shard_rows, key_parts, head_count, head_size) * shares[:, :, :, None]
    result = jnp.sum(pieces, axis=1).reshape(shard_rows, width)
    result = result.astype(jnp.bfloat16)
    return result

def run_copies(pairs, sem):
    copies = [pltpu.make_async_copy(a, b, sem.at[i]) for i, (a, b) in enumerate(pairs)]
    for copy in copies:
        copy.start()
    return copies


def aligned(index, size):
    return pl.ds(pl.multiple_of(index * size, size), size)


def pack_kernel(chunk, queries, keys, values, pair, to_1, to_2, to_3, sem):
    column = lax.axis_index("pb")
    half = lax.axis_index("ka") % 2
    heads = keys.shape[1] // HEAD_DIM
    theirs = aligned((1 - half) * 2 + chunk, HEAD_DIM)
    pairs = [(keys.at[:, theirs], pair.at[0]), (values.at[:, theirs], pair.at[1])]
    for d, to in ((1, to_1), (2, to_2), (3, to_3)):
        pairs.append((queries.at[:, aligned((column ^ d) * heads + half * 2 + chunk, HEAD_DIM)], to))
    for copy in run_copies(pairs, sem):
        copy.wait()


def pack(chunk, queries, keys, values):
    pair = jax.ShapeDtypeStruct((2, keys.shape[0], HEAD_DIM), keys.dtype)
    head = jax.ShapeDtypeStruct((queries.shape[0], HEAD_DIM), queries.dtype)
    return pl.pallas_call(
        functools.partial(pack_kernel, chunk),
        out_shape=[pair] + [head] * 3,
        in_specs=[pl.BlockSpec(memory_space=pltpu.HBM)] * 3,
        out_specs=[VMEM] * 4,
        scratch_shapes=[pltpu.SemaphoreType.DMA((5,))],
        name="pack",
    )(queries, keys, values)


def attend_kernel(chunk, scale, steps_ref, queries, keys, values, q_1, q_2, q_3, got, own, to_1, to_2, to_3,
                  q_buf, k_buf, v_buf, stats_buf, parts, sem, out_sem):
    column = lax.axis_index("pb")
    z = lax.axis_index("ka")
    rows = queries.shape[0]
    half_rows, sub = rows // 2, rows // 4
    held = keys.shape[0]
    pair = 2 * held
    heads = keys.shape[1] // HEAD_DIM
    upper, half = z // 2, z % 2
    left = pl.ds(0, HEAD_DIM)
    head = aligned(half * 2 + chunk, HEAD_DIM)

    def place(block):
        return (block + 4 - 2 * upper) % 4

    pairs = [
        (keys.at[:, head], k_buf.at[aligned(half, held), :]),
        (got.at[0], k_buf.at[aligned(1 - half, held), :]),
        (queries.at[:, aligned(column * heads + half * 2 + chunk, HEAD_DIM)], q_buf.at[place(column)]),
    ]
    pairs += [(q, q_buf.at[place(column ^ d)]) for d, q in ((1, q_1), (2, q_2), (3, q_3))]
    pairs += [
        (values.at[:, head], v_buf.at[aligned(half, held), left]),
        (got.at[1], v_buf.at[aligned(1 - half, held), left]),
    ]
    copies = run_copies(pairs, sem)
    v_buf[:, HEAD_DIM:] = jnp.ones((pair, HEAD_DIM), jnp.bfloat16)
    steps = steps_ref[...].astype(jnp.float32)
    columns = jnp.transpose(steps)
    for copy in copies:
        copy.wait()

    def tile(slot, start, first_row, limit, masked_from, base, stats, size=half_rows):
        scores = lax.dot_general(q_buf[slot, start:start + size, :], k_buf[:limit, :],
                                 (((1,), (1,)), ((), ())), preferred_element_type=jnp.float32)
        if masked_from < limit:
            at = (first_row + start) // LANES
            q_steps = jnp.concatenate([columns[:, g:g + 1] for g in range(at, at + size // LANES)], axis=0)
            k_steps = jnp.concatenate([steps[g:g + 1] for g in range((base + masked_from) // LANES, (base + limit) // LANES)], axis=1)
            seen = jnp.where(k_steps <= q_steps, scores[:, masked_from:], UNSEEN / scale)
            scores = jnp.concatenate([scores[:, :masked_from], seen], axis=1) if masked_from else seen
        top = jnp.max(scores, axis=1, keepdims=True) * scale
        top = top.astype(jnp.bfloat16).astype(jnp.float32)
        weights = jnp.exp2(scores * scale - top).astype(jnp.bfloat16)
        mixed = lax.dot_general(weights, v_buf[:limit, :], (((1,), (0,)), ((), ())), preferred_element_type=jnp.float32)
        total = mixed[:, HEAD_DIM:]
        result = (mixed[:, :HEAD_DIM] / total).astype(jnp.bfloat16)
        for j in range(0, size, sub):
            parts[(start + j) // sub, slot * sub:(slot + 1) * sub, :] = result[j:j + sub]
        high = total.astype(jnp.bfloat16).astype(jnp.float32)
        lane = lax.broadcasted_iota(jnp.int32, (size, LANES), 1)
        stats = jnp.where(lane == 3 * slot, top, stats)
        stats = jnp.where(lane == 3 * slot + 1, high, stats)
        return jnp.where(lane == 3 * slot + 2, total - high, stats)

    def region(which, start):
        base = which * pair
        reach = start + half_rows + LANES
        stats = jnp.zeros((half_rows, LANES), jnp.float32)
        stats = tile(0, start, base, reach, start, base, stats)
        stats = tile(1, start, base + held, min(held + reach, pair), held + start, base, stats)
        if which == 0:
            stats = tile(2, start, 0, pair, pair, base, stats)
            stats = tile(3, start, 0, pair, pair, base, stats)
        stats_buf[...] = stats
        if which == 1 and start > 0:
            stats_buf[sub:, :] = tile(3, start + sub, held, LANES, 0, base, stats[sub:], sub)
        for j in range(2):
            stats = jnp.transpose(stats_buf[j * sub:(j + 1) * sub, :])
            parts[start // sub + j, 4 * sub:, :] = stats[:STATS].astype(jnp.bfloat16)

    def send(outs):
        copies = [pltpu.make_async_copy(parts.at[z ^ d], to, out_sem.at[d]) for d, to in outs]
        for copy in copies:
            copy.start()
        return copies

    for which in range(2):
        @pl.when(upper == which)
        def _():
            region(which, (1 - which) * half_rows)

    sent = send(((3, to_3), (2, to_2)))
    for which in range(2):
        @pl.when(upper == which)
        def _():
            region(which, which * half_rows)

    for copy in sent + send(((1, to_1), (0, own))):
        copy.wait()


def attend(chunk, steps, queries, keys, values, ready):
    rows = queries.shape[0]
    held = keys.shape[0]
    part = jax.ShapeDtypeStruct((rows + STATS, LANES), jnp.bfloat16)
    exps = 4 * rows * 2 * held
    return pl.pallas_call(
        functools.partial(attend_kernel, chunk, math.log2(math.e) / math.sqrt(HEAD_DIM)),
        out_shape=[part] * 4,
        in_specs=[VMEM] + [ANY] * 7,
        out_specs=[ANY] * 4,
        scratch_shapes=[
            pltpu.VMEM((4, rows, HEAD_DIM), jnp.bfloat16),
            pltpu.VMEM((2 * held, HEAD_DIM), jnp.bfloat16),
            pltpu.VMEM((2 * held, 2 * HEAD_DIM), jnp.bfloat16),
            pltpu.VMEM((rows // 2, LANES), jnp.float32),
            pltpu.VMEM((4,) + part.shape, jnp.bfloat16),
            pltpu.SemaphoreType.DMA((8,)),
            pltpu.SemaphoreType.DMA((4,)),
        ],
        compiler_params=pltpu.CompilerParams(vmem_limit_bytes=24 << 20),
        cost_estimate=pl.CostEstimate(flops=exps * 4 * HEAD_DIM, bytes_accessed=4 << 20, transcendentals=exps),
        name="attend",
    )(steps, queries, keys, values, *ready)


def merge_kernel(own, from_1, from_2, from_3, out_0, out_1, out_2, out_3, held, result, sem):
    column = lax.axis_index("pb")
    z = lax.axis_index("ka")
    sub = result.shape[2]
    for copy in run_copies([(a, held.at[z ^ d]) for d, a in enumerate((own, from_1, from_2, from_3))], sem):
        copy.wait()
    stats = [jnp.transpose(held[s, 4 * sub:, :].astype(jnp.float32)) for s in range(4)]

    def part(s, slot):
        return held[s, slot * sub:(slot + 1) * sub, :]

    def merge_block(block, half):
        parts = ((half, block), (2 + half, (block + 2) % 4))
        tops = [stats[s][:, 3 * slot:3 * slot + 1] for s, slot in parts]
        totals = [stats[s][:, 3 * slot + 1:3 * slot + 2] + stats[s][:, 3 * slot + 2:3 * slot + 3] for s, slot in parts]
        best = jnp.maximum(*tops)
        shares = [total * jnp.exp2(top - best) for top, total in zip(tops, totals)]
        share = shares[0] / (shares[0] + shares[1])
        a, b = [part(s, slot).astype(jnp.float32) for s, slot in parts]
        result[block, half] = (a * share + b * (1.0 - share)).astype(jnp.bfloat16)

    for half in range(2):
        result[0, half] = part(half, 0)
        merge_block(2, half)
        merge_block(3, half)

    @pl.when(z < 3)
    def _():
        for half in range(2):
            result[1, half] = part(half, 1)

    @pl.when(z == 3)
    def _():
        for half in range(2):
            merge_block(1, half)

    outs = ((3, out_3), (2, out_2), (1, out_1), (0, out_0))
    for copy in run_copies([(result.at[column ^ d], out) for d, out in outs], sem):
        copy.wait()


def merge(parts):
    sub = (parts[0].shape[0] - STATS) // 4
    block = jax.ShapeDtypeStruct((2, sub, HEAD_DIM), jnp.bfloat16)
    return pl.pallas_call(
        merge_kernel,
        out_shape=[block] * 4,
        in_specs=[ANY] * 4,
        out_specs=[ANY] * 4,
        scratch_shapes=[
            pltpu.VMEM((4,) + parts[0].shape, jnp.bfloat16),
            pltpu.VMEM((4,) + block.shape, jnp.bfloat16),
            pltpu.SemaphoreType.DMA((4,)),
        ],
        compiler_params=pltpu.CompilerParams(vmem_limit_bytes=4 << 20),
        cost_estimate=pl.CostEstimate(flops=1 << 10, bytes_accessed=1 << 10, transcendentals=0),
        name="merge",
    )(*parts)


def assemble_kernel(*refs):
    pieces, (out, held, sem) = refs[:-3], refs[-3:]
    column = lax.axis_index("pb")
    pairs = []
    for i, piece in enumerate(pieces):
        chunk, d = i // 4, i % 4
        pairs += [(piece.at[half], held.at[(column ^ d) * 4 + 2 * half + chunk]) for half in range(2)]
    for copy in run_copies(pairs, sem):
        copy.wait()
    for head in range(held.shape[0]):
        out[:, head * HEAD_DIM:(head + 1) * HEAD_DIM] = held[head]


def assemble(pieces):
    sub = pieces[0].shape[1]
    return pl.pallas_call(
        assemble_kernel,
        out_shape=jax.ShapeDtypeStruct((sub, 16 * HEAD_DIM), jnp.bfloat16),
        in_specs=[ANY] * 8,
        out_specs=VMEM,
        scratch_shapes=[pltpu.VMEM((16, sub, HEAD_DIM), jnp.bfloat16), pltpu.SemaphoreType.DMA((16,))],
        compiler_params=pltpu.CompilerParams(vmem_limit_bytes=4 << 20),
        name="assemble",
    )(*pieces)


def by_pairs(queries, keys, values, step_of):
    steps = step_of.reshape(-1, LANES)
    swaps = [[(i, i ^ d) for i in range(4)] for d in range(4)]
    ready = []
    for chunk in range(2):
        pair, *sent = pack(chunk, queries, keys, values)
        got = lax.ppermute(pair, "ka", swaps[1])
        ready.append([lax.ppermute(piece, "pb", swap) for piece, swap in zip(sent, swaps[1:])] + [got])
    pieces = []
    for chunk in range(2):
        own, *parts = attend(chunk, steps, queries, keys, values, ready[chunk])
        blocks = merge([own] + [lax.ppermute(part, "ka", swap) for part, swap in zip(parts, swaps[1:])])
        pieces += [blocks[0]] + [lax.ppermute(piece, "pb", swap) for piece, swap in zip(blocks[1:], swaps[1:])]
    return assemble(pieces)


def on_device(queries, keys, values, step_of):
    rows = queries.shape[0]
    held, block = keys.shape
    square = (
        lax.axis_size("pb") == 4
        and lax.axis_size("ka") == 4
        and held == rows == 4 * LANES
        and block == 4 * HEAD_DIM
    )
    if square:
        return by_pairs(queries, keys, values, step_of)
    return on_any(queries, keys, values, step_of)


def solution(mesh):
    placed = (
        P(("groups", "pb"), None),
        P(("groups", "ka"), "pb"),
        P(("groups", "ka"), "pb"),
        P("groups"),
    )
    return jax.shard_map(
        on_device,
        mesh=mesh,
        in_specs=placed,
        out_specs=P(("groups", "pb", "ka"), None),
        check_vma=False,
    )
```

```python
import functools
import math

import jax
import jax.numpy as jnp
from jax import lax
from jax.experimental import pallas as pl
from jax.experimental.pallas import tpu as pltpu
from jax.sharding import PartitionSpec as P

HEAD_DIM = 128
LANES = 128
LOW_SCORE = -1e30
UNSEEN = -float(1 << 20)
ROW_TILE = 256
STATS = 16
ANY = pl.BlockSpec(memory_space=pl.ANY)
VMEM = pl.BlockSpec(memory_space=pltpu.VMEM)


def attend_half(q_rows, q_steps, keys_all, values_all, key_steps, block_keys):
    row_count, width = q_rows.shape
    head_size = HEAD_DIM
    head_count = width // head_size
    key_count = keys_all.shape[0]
    block_count = key_count // block_keys
    factor_scale = 1.0 / math.sqrt(head_size)
    q_heads = q_rows.reshape(row_count, head_count, head_size)
    blocks = (
        keys_all.reshape(block_count, block_keys, head_count, head_size),
        values_all.reshape(block_count, block_keys, head_count, head_size),
        key_steps.reshape(block_count, block_keys),
    )
    last_step = q_steps[row_count - 1]

    def compute(carry, key_block, value_block, step_block):
        run_max, run_sum, run_out = carry
        scores = (
            jnp.einsum("rhd,khd->hkr", q_heads, key_block, preferred_element_type=jnp.float32)
            * factor_scale
        )
        visible = step_block[None, :, None] <= q_steps[None, None, :]
        masked = jnp.where(visible, scores, LOW_SCORE)
        new_max = jnp.maximum(run_max, jnp.max(masked, axis=1))
        weights = jnp.where(visible, jnp.exp(masked - new_max[:, None, :]), 0.0)
        rescale = jnp.exp(run_max - new_max)
        new_sum = run_sum * rescale + jnp.sum(weights, axis=1)
        update = jnp.einsum(
            "hkr,khd->rhd",
            weights.astype(jnp.bfloat16),
            value_block,
            preferred_element_type=jnp.float32,
        )
        new_out = run_out * jnp.transpose(rescale)[:, :, None] + update
        return (new_max, new_sum, new_out)

    def visit(carry, block):
        key_block, value_block, step_block = block
        result = lax.cond(
            step_block[0] <= last_step,
            lambda state: compute(state, key_block, value_block, step_block),
            lambda state: state,
            carry,
        )
        return (result, None)

    initial = (
        jnp.full((head_count, row_count), LOW_SCORE, jnp.float32),
        jnp.zeros((head_count, row_count), jnp.float32),
        jnp.zeros((row_count, head_count, head_size), jnp.float32),
    )
    final_state, unused = lax.scan(visit, initial, blocks)
    return final_state


def on_any(queries, keys, values, step_of):
    block_rows, width = queries.shape
    head_size = HEAD_DIM
    head_count = width // head_size
    key_parts = lax.axis_size("ka")
    query_index = lax.axis_index("pb")
    key_index = lax.axis_index("ka")
    shard_rows = block_rows // key_parts
    half_rows = block_rows // 2
    key_count = keys.shape[0]
    first_steps = lax.dynamic_slice_in_dim(step_of, query_index * block_rows, half_rows)
    second_steps = lax.dynamic_slice_in_dim(
        step_of, query_index * block_rows + half_rows, half_rows
    )
    keys_mine, values_mine = (keys, values)
    key_steps = lax.dynamic_slice_in_dim(step_of, key_index * key_count, key_count)
    keys_all, values_all = (
        lax.all_gather(keys_mine, "pb", axis=1, tiled=True),
        lax.all_gather(values_mine, "pb", axis=1, tiled=True),
    )
    block_keys = math.gcd(64, key_count)
    first_state = attend_half(
        queries[:half_rows], first_steps, keys_all, values_all, key_steps, block_keys
    )
    second_state = attend_half(
        queries[half_rows:], second_steps, keys_all, values_all, key_steps, block_keys
    )
    row_max = jnp.concatenate([first_state[0], second_state[0]], axis=1)
    row_sum = jnp.concatenate([first_state[1], second_state[1]], axis=1)
    row_out = jnp.concatenate([first_state[2], second_state[2]], axis=0)
    sent = (
        jnp.transpose(row_max)[:, None, :],
        jnp.transpose(row_sum)[:, None, :],
        row_out.reshape(block_rows, 1, width),
    )
    got_max, got_sum, got_out = (
        lax.all_to_all(sent[0], "ka", split_axis=0, concat_axis=1, tiled=True),
        lax.all_to_all(sent[1], "ka", split_axis=0, concat_axis=1, tiled=True),
        lax.all_to_all(sent[2], "ka", split_axis=0, concat_axis=1, tiled=True),
    )
    best = jnp.max(got_max, axis=1, keepdims=True)
    weight = jnp.exp(got_max - best)
    total = jnp.sum(got_sum * weight, axis=1)
    shares = weight / total[:, None, :]
    pieces = got_out.reshape(shard_rows, key_parts, head_count, head_size) * shares[:, :, :, None]
    result = jnp.sum(pieces, axis=1).reshape(shard_rows, width)
    result = result.astype(jnp.bfloat16)
    return result

def run_copies(pairs, sem):
    copies = [pltpu.make_async_copy(a, b, sem.at[i]) for i, (a, b) in enumerate(pairs)]
    for copy in copies:
        copy.start()
    return copies


def aligned(index, size):
    return pl.ds(pl.multiple_of(index * size, size), size)


def region_of(z, far):
    return 1 - z // 2 if far else z // 2


def pack_kernel(batches, queries, keys, values, *refs):
    outs, sem = refs[:-1], refs[-1]
    column = lax.axis_index("pb")
    z = lax.axis_index("ka")
    half = z % 2
    heads = keys.shape[1] // HEAD_DIM
    count = queries.shape[0] // 2
    pairs = []
    for chunk, to in enumerate(outs[:2]):
        theirs = aligned((1 - half) * 2 + chunk, HEAD_DIM)
        pairs += [(keys.at[:, theirs], to.at[0]), (values.at[:, theirs], to.at[1])]
    for b, batch in enumerate(batches):
        for i, (chunk, far) in enumerate(batch):
            for d, to in zip((1, 2, 3), outs[2 + 3 * b:]):
                cut = (aligned(region_of(z, far), count), aligned((column ^ d) * heads + half * 2 + chunk, HEAD_DIM))
                pairs.append((queries.at[cut], to.at[pl.ds(i * count, count), :]))
    for copy in run_copies(pairs, sem):
        copy.wait()


def pack(batches, queries, keys, values):
    pair = jax.ShapeDtypeStruct((2, keys.shape[0], HEAD_DIM), keys.dtype)
    rows = [jax.ShapeDtypeStruct((len(batch) * queries.shape[0] // 2, HEAD_DIM), queries.dtype) for batch in batches]
    return pl.pallas_call(
        functools.partial(pack_kernel, batches),
        out_shape=[pair] * 2 + sum([[shape] * 3 for shape in rows], []),
        in_specs=[ANY] * 3,
        out_specs=[VMEM] * (2 + 3 * len(batches)),
        scratch_shapes=[pltpu.SemaphoreType.DMA((4 + 3 * sum(map(len, batches)),))],
        name="pack",
    )(queries, keys, values)


def attend_kernel(shapes, skip, waits, scale, steps_ref, queries, keys, values, *refs):
    refs = refs[waits:]
    chunks = sorted({chunk for chunk, _ in shapes})
    count = len(shapes)
    moved, got = refs[:3], refs[3:3 + len(chunks)]
    outs = refs[3 + len(chunks):3 + len(chunks) + 2 * count]
    q_buf, k_buf, v_buf, stats_buf, parts, sem, out_sem = refs[3 + len(chunks) + 2 * count:]
    column = lax.axis_index("pb")
    z = lax.axis_index("ka")
    half_rows = queries.shape[0] // 2
    sub = half_rows // 2
    held = keys.shape[0]
    pair = 2 * held
    heads = keys.shape[1] // HEAD_DIM
    upper, half = z // 2, z % 2
    left = pl.ds(0, HEAD_DIM)

    def place(block):
        return (block + 4 - 2 * upper) % 4

    pairs = []
    for i, chunk in enumerate(chunks):
        head = aligned(half * 2 + chunk, HEAD_DIM)
        pairs += [
            (keys.at[:, head], k_buf.at[i, aligned(half, held), :]),
            (got[i].at[0], k_buf.at[i, aligned(1 - half, held), :]),
            (values.at[:, head], v_buf.at[i, aligned(half, held), left]),
            (got[i].at[1], v_buf.at[i, aligned(1 - half, held), left]),
        ]
    for i, (chunk, far) in enumerate(shapes):
        cut = (aligned(region_of(z, far), half_rows), aligned(column * heads + half * 2 + chunk, HEAD_DIM))
        pairs.append((queries.at[cut], q_buf.at[i, place(column)]))
        for d, q in zip((1, 2, 3), moved):
            pairs.append((q.at[pl.ds((skip + i) * half_rows, half_rows), :], q_buf.at[i, place(column ^ d)]))
    copies = run_copies(pairs, sem)
    v_buf[:, :, HEAD_DIM:] = jnp.ones((len(chunks), pair, HEAD_DIM), jnp.bfloat16)
    steps = steps_ref[...].astype(jnp.float32)
    columns = jnp.transpose(steps)
    for copy in copies:
        copy.wait()

    def region(i, which):
        chunk, far = shapes[i]
        kv = chunks.index(chunk)
        start = half_rows if far == (which == 0) else 0
        base = which * pair

        def tile(slot, first_row, limit, masked_from, stats, first=0, size=half_rows):
            scores = lax.dot_general(q_buf[i, slot, first:first + size, :], k_buf[kv, :limit, :],
                                     (((1,), (1,)), ((), ())), preferred_element_type=jnp.float32)
            if masked_from < limit:
                at = (first_row + first) // LANES
                q_steps = jnp.concatenate([columns[:, g:g + 1] for g in range(at, at + size // LANES)], axis=0)
                k_steps = jnp.concatenate(
                    [steps[g:g + 1] for g in range((base + masked_from) // LANES, (base + limit) // LANES)], axis=1)
                seen = jnp.where(k_steps <= q_steps, scores[:, masked_from:], UNSEEN / scale)
                scores = jnp.concatenate([scores[:, :masked_from], seen], axis=1) if masked_from else seen
            top = jnp.max(scores, axis=1, keepdims=True) * scale
            top = top.astype(jnp.bfloat16).astype(jnp.float32)
            weights = jnp.exp2(scores * scale - top).astype(jnp.bfloat16)
            mixed = lax.dot_general(weights, v_buf[kv, :limit, :], (((1,), (0,)), ((), ())), preferred_element_type=jnp.float32)
            total = mixed[:, HEAD_DIM:]
            result = (mixed[:, :HEAD_DIM] / total).astype(jnp.bfloat16)
            for j in range(0, size, sub):
                parts[i, (first + j) // sub, slot * sub:(slot + 1) * sub, :] = result[j:j + sub]
            high = total.astype(jnp.bfloat16).astype(jnp.float32)
            lane = lax.broadcasted_iota(jnp.int32, (size, LANES), 1)
            stats = jnp.where(lane == 3 * slot, top, stats)
            stats = jnp.where(lane == 3 * slot + 1, high, stats)
            return jnp.where(lane == 3 * slot + 2, total - high, stats)

        reach = start + half_rows + LANES
        stats = jnp.zeros((half_rows, LANES), jnp.float32)
        stats = tile(0, base + start, reach, start, stats)
        stats = tile(1, base + held + start, min(held + reach, pair), held + start, stats)
        if which == 0:
            stats = tile(2, 0, pair, pair, stats)
            stats = tile(3, 0, pair, pair, stats)
        stats_buf[...] = stats
        if which == 1 and not far:
            stats_buf[sub:, :] = tile(3, held + start, LANES, 0, stats[sub:], sub, sub)
        for j in range(2):
            stats = jnp.transpose(stats_buf[j * sub:(j + 1) * sub, :])
            parts[i, j, 4 * sub:, :] = stats[:STATS].astype(jnp.bfloat16)

    sent = []
    for i in range(count):
        for which in range(2):
            pl.when(upper == which)(functools.partial(region, i, which))
        for j, place_in_pair in enumerate((half, 1 - half)):
            copy = pltpu.make_async_copy(parts.at[i, place_in_pair], outs[2 * i + j], out_sem.at[2 * i + j])
            copy.start()
            sent.append(copy)
    for copy in sent:
        copy.wait()


def attend(shapes, skip, steps, queries, keys, values, moved, got, after=()):
    chunks = len({chunk for chunk, _ in shapes})
    count = len(shapes)
    rows = queries.shape[0]
    held = keys.shape[0]
    part = jax.ShapeDtypeStruct((rows + STATS, LANES), jnp.bfloat16)
    return pl.pallas_call(
        functools.partial(attend_kernel, shapes, skip, len(after), math.log2(math.e) / math.sqrt(HEAD_DIM)),
        out_shape=[part] * (2 * count),
        in_specs=[VMEM] + [ANY] * (6 + chunks + len(after)),
        out_specs=[ANY] * (2 * count),
        scratch_shapes=[
            pltpu.VMEM((count, 4, rows // 2, HEAD_DIM), jnp.bfloat16),
            pltpu.VMEM((chunks, 2 * held, HEAD_DIM), jnp.bfloat16),
            pltpu.VMEM((chunks, 2 * held, 2 * HEAD_DIM), jnp.bfloat16),
            pltpu.VMEM((rows // 2, LANES), jnp.float32),
            pltpu.VMEM((count, 2) + part.shape, jnp.bfloat16),
            pltpu.SemaphoreType.DMA((4 * chunks + 4 * count,)),
            pltpu.SemaphoreType.DMA((2 * count,)),
        ],
        compiler_params=pltpu.CompilerParams(vmem_limit_bytes=24 << 20),
        cost_estimate=pl.CostEstimate(flops=1 << 10, bytes_accessed=1 << 10, transcendentals=0),
        name="attend_far" if shapes[0][1] else "attend_near",
    )(steps, queries, keys, values, *after, *moved, *got)


def collect_kernel(a, b, out, sem):
    for copy in run_copies([(a, out.at[0]), (b, out.at[1])], sem):
        copy.wait()


def collect(a, b):
    return pl.pallas_call(
        collect_kernel,
        out_shape=jax.ShapeDtypeStruct((2,) + a.shape, a.dtype),
        in_specs=[ANY] * 2,
        out_specs=ANY,
        scratch_shapes=[pltpu.SemaphoreType.DMA((2,))],
        compiler_params=pltpu.CompilerParams(vmem_limit_bytes=4 << 20),
        cost_estimate=pl.CostEstimate(flops=1 << 30, bytes_accessed=32 << 20, transcendentals=0),
        name="collect",
    )(a, b)


def merge_kernel(waits, *refs):
    own, from_1, *far = refs[waits:-7]
    (out_0, out_1, out_2, out_3, held, result, sem) = refs[-7:]
    if len(far) == 1:
        far = (far[0].at[0], far[0].at[1])
    column = lax.axis_index("pb")
    z = lax.axis_index("ka")
    sub = result.shape[2]
    for copy in run_copies([(a, held.at[z ^ d]) for d, a in enumerate((own, from_1) + tuple(far))], sem):
        copy.wait()
    stats = [jnp.transpose(held[s, 4 * sub:, :].astype(jnp.float32)) for s in range(4)]

    def part(s, slot):
        return held[s, slot * sub:(slot + 1) * sub, :]

    def merge_block(block, half):
        parts = ((half, block), (2 + half, (block + 2) % 4))
        tops = [stats[s][:, 3 * slot:3 * slot + 1] for s, slot in parts]
        totals = [stats[s][:, 3 * slot + 1:3 * slot + 2] + stats[s][:, 3 * slot + 2:3 * slot + 3] for s, slot in parts]
        best = jnp.maximum(*tops)
        shares = [total * jnp.exp2(top - best) for top, total in zip(tops, totals)]
        share = shares[0] / (shares[0] + shares[1])
        a, b = [part(s, slot).astype(jnp.float32) for s, slot in parts]
        result[block, half] = (a * share + b * (1.0 - share)).astype(jnp.bfloat16)

    for half in range(2):
        result[0, half] = part(half, 0)
        merge_block(2, half)
        merge_block(3, half)

    @pl.when(z < 3)
    def _():
        for half in range(2):
            result[1, half] = part(half, 1)

    @pl.when(z == 3)
    def _():
        for half in range(2):
            merge_block(1, half)

    outs = ((3, out_3), (2, out_2), (1, out_1), (0, out_0))
    for copy in run_copies([(result.at[column ^ d], out) for d, out in outs], sem):
        copy.wait()


def merge(parts, after=()):
    sub = (parts[0].shape[0] - STATS) // 4
    block = jax.ShapeDtypeStruct((2, sub, HEAD_DIM), jnp.bfloat16)
    return pl.pallas_call(
        functools.partial(merge_kernel, len(after)),
        out_shape=[block] * 4,
        in_specs=[ANY] * (len(after) + len(parts)),
        out_specs=[ANY] * 4,
        scratch_shapes=[
            pltpu.VMEM((4,) + parts[0].shape, jnp.bfloat16),
            pltpu.VMEM((4,) + block.shape, jnp.bfloat16),
            pltpu.SemaphoreType.DMA((4,)),
        ],
        compiler_params=pltpu.CompilerParams(vmem_limit_bytes=4 << 20),
        cost_estimate=pl.CostEstimate(flops=1 << 10, bytes_accessed=1 << 10, transcendentals=0),
        name="merge",
    )(*after, *parts)


def assemble_kernel(chunk, *refs):
    pieces, (out, sem) = refs[-6:-2], refs[-2:]
    column = lax.axis_index("pb")
    pairs = []
    for d, piece in enumerate(pieces):
        for half in range(2):
            pairs.append((piece.at[half], out.at[:, aligned((column ^ d) * 4 + 2 * half + chunk, HEAD_DIM)]))
    for copy in run_copies(pairs, sem):
        copy.wait()


def assemble(chunk, pieces, begun=()):
    sub = pieces[0].shape[1]
    return pl.pallas_call(
        functools.partial(assemble_kernel, chunk),
        out_shape=jax.ShapeDtypeStruct((sub, 16 * HEAD_DIM), jnp.bfloat16),
        in_specs=[ANY] * (4 + len(begun)),
        out_specs=ANY,
        scratch_shapes=[pltpu.SemaphoreType.DMA((8,))],
        input_output_aliases={0: 0} if begun else {},
        compiler_params=pltpu.CompilerParams(vmem_limit_bytes=4 << 20),
        cost_estimate=pl.CostEstimate(flops=1 << 30, bytes_accessed=32 << 20, transcendentals=0),
        name="assemble",
    )(*begun, *pieces)


def by_pairs(queries, keys, values, step_of):
    steps = step_of.reshape(-1, LANES)
    swaps = [[(i, i ^ d) for i in range(4)] for d in range(4)]

    def travel(sent, axis):
        return [lax.ppermute(piece, axis, swap) for piece, swap in zip(sent, swaps[1:])]

    order = ((0, True), (0, False), (1, True), (1, False))
    packed = pack((order[:1], order[1:]), queries, keys, values)
    got = travel(packed[:1], "ka"), travel(packed[1:2], "ka")
    moved = travel(packed[2:5], "pb"), travel(packed[5:], "pb")
    parts = []
    for i, (chunk, far) in enumerate(order):
        after = [parts[-1][0]] if parts else []
        parts.append(attend((order[i],), max(i - 1, 0), steps, queries, keys, values, moved[min(i, 1)], got[chunk], after))
    far = [collect(lax.ppermute(same, "ka", swaps[2]), lax.ppermute(cross, "ka", swaps[3])) for same, cross in parts[::2]]
    result = ()
    blocks = ()
    for chunk, (own, beside) in enumerate(parts[1::2]):
        blocks = merge([own, lax.ppermute(beside, "ka", swaps[1]), far[chunk]], blocks[:1])
        result = (assemble(chunk, [blocks[0]] + travel(blocks[1:], "pb"), result),)
    return result[0]


def on_device(queries, keys, values, step_of):
    rows = queries.shape[0]
    held, block = keys.shape
    square = (
        lax.axis_size("pb") == 4
        and lax.axis_size("ka") == 4
        and held == rows == 4 * LANES
        and block == 4 * HEAD_DIM
    )
    if square:
        return by_pairs(queries, keys, values, step_of)
    return on_any(queries, keys, values, step_of)


def solution(mesh):
    placed = (
        P(("groups", "pb"), None),
        P(("groups", "ka"), "pb"),
        P(("groups", "ka"), "pb"),
        P("groups"),
    )
    return jax.shard_map(
        on_device,
        mesh=mesh,
        in_specs=placed,
        out_specs=P(("groups", "pb", "ka"), None),
        check_vma=False,
    )
```

```python
import functools
import math

import jax
import jax.numpy as jnp
from jax import lax
from jax.experimental import pallas as pl
from jax.experimental.pallas import tpu as pltpu
from jax.sharding import PartitionSpec as P

HEAD_DIM = 128
LANES = 128
LOW_SCORE = -1e30
UNSEEN = -float(1 << 20)
ROW_TILE = 256
STATS = 16
ANY = pl.BlockSpec(memory_space=pl.ANY)
VMEM = pl.BlockSpec(memory_space=pltpu.VMEM)


def attend_half(q_rows, q_steps, keys_all, values_all, key_steps, block_keys):
    row_count, width = q_rows.shape
    head_size = HEAD_DIM
    head_count = width // head_size
    key_count = keys_all.shape[0]
    block_count = key_count // block_keys
    factor_scale = 1.0 / math.sqrt(head_size)
    q_heads = q_rows.reshape(row_count, head_count, head_size)
    blocks = (
        keys_all.reshape(block_count, block_keys, head_count, head_size),
        values_all.reshape(block_count, block_keys, head_count, head_size),
        key_steps.reshape(block_count, block_keys),
    )
    last_step = q_steps[row_count - 1]

    def compute(carry, key_block, value_block, step_block):
        run_max, run_sum, run_out = carry
        scores = (
            jnp.einsum("rhd,khd->hkr", q_heads, key_block, preferred_element_type=jnp.float32)
            * factor_scale
        )
        visible = step_block[None, :, None] <= q_steps[None, None, :]
        masked = jnp.where(visible, scores, LOW_SCORE)
        new_max = jnp.maximum(run_max, jnp.max(masked, axis=1))
        weights = jnp.where(visible, jnp.exp(masked - new_max[:, None, :]), 0.0)
        rescale = jnp.exp(run_max - new_max)
        new_sum = run_sum * rescale + jnp.sum(weights, axis=1)
        update = jnp.einsum(
            "hkr,khd->rhd",
            weights.astype(jnp.bfloat16),
            value_block,
            preferred_element_type=jnp.float32,
        )
        new_out = run_out * jnp.transpose(rescale)[:, :, None] + update
        return (new_max, new_sum, new_out)

    def visit(carry, block):
        key_block, value_block, step_block = block
        result = lax.cond(
            step_block[0] <= last_step,
            lambda state: compute(state, key_block, value_block, step_block),
            lambda state: state,
            carry,
        )
        return (result, None)

    initial = (
        jnp.full((head_count, row_count), LOW_SCORE, jnp.float32),
        jnp.zeros((head_count, row_count), jnp.float32),
        jnp.zeros((row_count, head_count, head_size), jnp.float32),
    )
    final_state, unused = lax.scan(visit, initial, blocks)
    return final_state


def on_any(queries, keys, values, step_of):
    block_rows, width = queries.shape
    head_size = HEAD_DIM
    head_count = width // head_size
    key_parts = lax.axis_size("ka")
    query_index = lax.axis_index("pb")
    key_index = lax.axis_index("ka")
    shard_rows = block_rows // key_parts
    half_rows = block_rows // 2
    key_count = keys.shape[0]
    first_steps = lax.dynamic_slice_in_dim(step_of, query_index * block_rows, half_rows)
    second_steps = lax.dynamic_slice_in_dim(
        step_of, query_index * block_rows + half_rows, half_rows
    )
    keys_mine, values_mine = (keys, values)
    key_steps = lax.dynamic_slice_in_dim(step_of, key_index * key_count, key_count)
    keys_all, values_all = (
        lax.all_gather(keys_mine, "pb", axis=1, tiled=True),
        lax.all_gather(values_mine, "pb", axis=1, tiled=True),
    )
    block_keys = math.gcd(64, key_count)
    first_state = attend_half(
        queries[:half_rows], first_steps, keys_all, values_all, key_steps, block_keys
    )
    second_state = attend_half(
        queries[half_rows:], second_steps, keys_all, values_all, key_steps, block_keys
    )
    row_max = jnp.concatenate([first_state[0], second_state[0]], axis=1)
    row_sum = jnp.concatenate([first_state[1], second_state[1]], axis=1)
    row_out = jnp.concatenate([first_state[2], second_state[2]], axis=0)
    sent = (
        jnp.transpose(row_max)[:, None, :],
        jnp.transpose(row_sum)[:, None, :],
        row_out.reshape(block_rows, 1, width),
    )
    got_max, got_sum, got_out = (
        lax.all_to_all(sent[0], "ka", split_axis=0, concat_axis=1, tiled=True),
        lax.all_to_all(sent[1], "ka", split_axis=0, concat_axis=1, tiled=True),
        lax.all_to_all(sent[2], "ka", split_axis=0, concat_axis=1, tiled=True),
    )
    best = jnp.max(got_max, axis=1, keepdims=True)
    weight = jnp.exp(got_max - best)
    total = jnp.sum(got_sum * weight, axis=1)
    shares = weight / total[:, None, :]
    pieces = got_out.reshape(shard_rows, key_parts, head_count, head_size) * shares[:, :, :, None]
    result = jnp.sum(pieces, axis=1).reshape(shard_rows, width)
    result = result.astype(jnp.bfloat16)
    return result

def run_copies(pairs, sem):
    copies = [pltpu.make_async_copy(a, b, sem.at[i]) for i, (a, b) in enumerate(pairs)]
    for copy in copies:
        copy.start()
    return copies


def aligned(index, size):
    return pl.ds(pl.multiple_of(index * size, size), size)


def region_of(z, far):
    return 1 - z // 2 if far else z // 2


def pack_kernel(batches, queries, keys, values, *refs):
    outs, sem = refs[:-1], refs[-1]
    column = lax.axis_index("pb")
    z = lax.axis_index("ka")
    half = z % 2
    heads = keys.shape[1] // HEAD_DIM
    count = queries.shape[0] // 2
    pairs = []
    for chunk, to in enumerate(outs[:2]):
        theirs = aligned((1 - half) * 2 + chunk, HEAD_DIM)
        pairs += [(keys.at[:, theirs], to.at[0]), (values.at[:, theirs], to.at[1])]
    for b, batch in enumerate(batches):
        for i, (chunk, far) in enumerate(batch):
            for d, to in zip((1, 2, 3), outs[2 + 3 * b:]):
                cut = (aligned(region_of(z, far), count), aligned((column ^ d) * heads + half * 2 + chunk, HEAD_DIM))
                pairs.append((queries.at[cut], to.at[pl.ds(i * count, count), :]))
    for copy in run_copies(pairs, sem):
        copy.wait()


def pack(batches, queries, keys, values):
    pair = jax.ShapeDtypeStruct((2, keys.shape[0], HEAD_DIM), keys.dtype)
    rows = [jax.ShapeDtypeStruct((len(batch) * queries.shape[0] // 2, HEAD_DIM), queries.dtype) for batch in batches]
    return pl.pallas_call(
        functools.partial(pack_kernel, batches),
        out_shape=[pair] * 2 + sum([[shape] * 3 for shape in rows], []),
        in_specs=[ANY] * 3,
        out_specs=[VMEM] * (2 + 3 * len(batches)),
        scratch_shapes=[pltpu.SemaphoreType.DMA((4 + 3 * sum(map(len, batches)),))],
        name="pack",
    )(queries, keys, values)


def attend_kernel(chunk, far, skip, waits, scale, steps_ref, queries, keys, values, *refs):
    *moved, got, same, cross, q_buf, k_buf, v_buf = refs[waits:]
    column = lax.axis_index("pb")
    z = lax.axis_index("ka")
    half_rows = q_buf.shape[1]
    sub = half_rows // 2
    held = keys.shape[0]
    pair = 2 * held

    def sort_queries(mine):
        for d, q in zip((1, 2, 3), moved):
            q_buf[mine ^ d] = q[skip * half_rows:(skip + 1) * half_rows, :]

    def work(which):
        upper, half = which // 2, which % 2
        start = half_rows if far == (upper == 0) else 0
        base = upper * pair
        outs = (same, cross) if half == 0 else (cross, same)

        def own_queries(mine):
            at = (mine * 4 + half * 2 + chunk) * HEAD_DIM
            q_buf[mine] = queries[start:start + half_rows, at:at + HEAD_DIM]

        for mine in range(4):
            pl.when(column == mine)(functools.partial(own_queries, mine))
        head = slice((half * 2 + chunk) * HEAD_DIM, (half * 2 + chunk + 1) * HEAD_DIM)
        for buf, own, theirs in ((k_buf, keys, got.at[0]), (v_buf, values, got.at[1])):
            buf[half * held:(half + 1) * held, :HEAD_DIM] = own[:, head]
            buf[(1 - half) * held:(2 - half) * held, :HEAD_DIM] = theirs[...]
        v_buf[:, HEAD_DIM:] = jnp.ones((pair, HEAD_DIM), jnp.bfloat16)
        steps = steps_ref[...].astype(jnp.float32)
        columns = jnp.transpose(steps)

        def tile(slot, first_row, limit, masked_from, stats, first=0, size=half_rows):
            q = q_buf[(slot + 2 * upper) % 4, first:first + size, :]
            scores = lax.dot_general(q, k_buf[:limit, :], (((1,), (1,)), ((), ())), preferred_element_type=jnp.float32)
            if masked_from < limit:
                at = (first_row + first) // LANES
                q_steps = jnp.concatenate([columns[:, g:g + 1] for g in range(at, at + size // LANES)], axis=0)
                k_steps = jnp.concatenate(
                    [steps[g:g + 1] for g in range((base + masked_from) // LANES, (base + limit) // LANES)], axis=1)
                seen = jnp.where(k_steps <= q_steps, scores[:, masked_from:], UNSEEN / scale)
                scores = jnp.concatenate([scores[:, :masked_from], seen], axis=1) if masked_from else seen
            top = jnp.max(scores, axis=1, keepdims=True) * scale
            top = top.astype(jnp.bfloat16).astype(jnp.float32)
            weights = jnp.exp2(scores * scale - top).astype(jnp.bfloat16)
            mixed = lax.dot_general(weights, v_buf[:limit, :], (((1,), (0,)), ((), ())), preferred_element_type=jnp.float32)
            total = mixed[:, HEAD_DIM:]
            result = (mixed[:, :HEAD_DIM] / total).astype(jnp.bfloat16)
            for j in range(0, size, sub):
                outs[(first + j) // sub][slot * sub:(slot + 1) * sub, :] = result[j:j + sub]
            high = total.astype(jnp.bfloat16).astype(jnp.float32)
            lane = lax.broadcasted_iota(jnp.int32, (size, LANES), 1)
            stats = jnp.where(lane == 3 * slot, top, stats)
            stats = jnp.where(lane == 3 * slot + 1, high, stats)
            return jnp.where(lane == 3 * slot + 2, total - high, stats)

        reach = start + half_rows + LANES
        stats = jnp.zeros((half_rows, LANES), jnp.float32)
        stats = tile(0, base + start, reach, start, stats)
        stats = tile(1, base + held + start, min(held + reach, pair), held + start, stats)
        if upper == 0:
            stats = tile(2, 0, pair, pair, stats)
            stats = tile(3, 0, pair, pair, stats)
        stats = [stats[:sub], stats[sub:]]
        if upper == 1 and not far:
            stats[1] = tile(3, held + start, LANES, 0, stats[1], sub, sub)
        for out, of in zip(outs, stats):
            out[4 * sub:, :] = jnp.transpose(of)[:STATS].astype(jnp.bfloat16)

    for which in range(4):
        pl.when(column == which)(functools.partial(sort_queries, which))
    for which in range(4):
        pl.when(z == which)(functools.partial(work, which))


def attend(chunk, far, skip, steps, queries, keys, values, moved, got, after=()):
    held = keys.shape[0]
    part = jax.ShapeDtypeStruct((held + STATS, LANES), jnp.bfloat16)
    return pl.pallas_call(
        functools.partial(attend_kernel, chunk, far, skip, len(after), math.log2(math.e) / math.sqrt(HEAD_DIM)),
        out_shape=[part] * 2,
        in_specs=[VMEM] * 4 + [ANY] * len(after) + [VMEM] * 4,
        out_specs=[VMEM] * 2,
        scratch_shapes=[
            pltpu.VMEM((4, held // 2, HEAD_DIM), jnp.bfloat16),
            pltpu.VMEM((2 * held, HEAD_DIM), jnp.bfloat16),
            pltpu.VMEM((2 * held, 2 * HEAD_DIM), jnp.bfloat16),
        ],
        compiler_params=pltpu.CompilerParams(vmem_limit_bytes=24 << 20),
        cost_estimate=pl.CostEstimate(flops=1 << 10, bytes_accessed=1 << 10, transcendentals=0),
        name="attend_far" if far else "attend_near",
    )(steps, queries, keys, values, *after, *moved, *got)


def collect_kernel(a, b, out, sem):
    for copy in run_copies([(a, out.at[0]), (b, out.at[1])], sem):
        copy.wait()


def collect(a, b):
    return pl.pallas_call(
        collect_kernel,
        out_shape=jax.ShapeDtypeStruct((2,) + a.shape, a.dtype),
        in_specs=[ANY] * 2,
        out_specs=ANY,
        scratch_shapes=[pltpu.SemaphoreType.DMA((2,))],
        compiler_params=pltpu.CompilerParams(vmem_limit_bytes=4 << 20),
        cost_estimate=pl.CostEstimate(flops=1 << 30, bytes_accessed=32 << 20, transcendentals=0),
        name="collect",
    )(a, b)


def merge_kernel(waits, *refs):
    own, from_1, far = refs[waits:waits + 3]
    outs, result = refs[waits + 3:-1], refs[-1]
    column = lax.axis_index("pb")
    z = lax.axis_index("ka")
    sub = result.shape[2]
    arrived = (own, from_1, far.at[0], far.at[1])

    def merge_at(which):
        held = [arrived[which ^ s] for s in range(4)]
        stats = [jnp.transpose(held[s][4 * sub:, :].astype(jnp.float32)) for s in range(4)]

        def part(s, slot):
            return held[s][slot * sub:(slot + 1) * sub, :]

        for half in range(2):
            for block in range(4):
                if block == 0 or block == 1 and which < 3:
                    result[block, half] = part(half, block)
                    continue
                parts = ((half, block), (2 + half, (block + 2) % 4))
                tops = [stats[s][:, 3 * slot:3 * slot + 1] for s, slot in parts]
                totals = [stats[s][:, 3 * slot + 1:3 * slot + 2] + stats[s][:, 3 * slot + 2:3 * slot + 3] for s, slot in parts]
                best = jnp.maximum(*tops)
                shares = [total * jnp.exp2(top - best) for top, total in zip(tops, totals)]
                share = shares[0] / (shares[0] + shares[1])
                a, b = [part(s, slot).astype(jnp.float32) for s, slot in parts]
                result[block, half] = (a * share + b * (1.0 - share)).astype(jnp.bfloat16)

    def sort_at(which):
        for d, out in enumerate(outs):
            out[...] = result[which ^ d]

    for which in range(4):
        pl.when(z == which)(functools.partial(merge_at, which))
    for which in range(4):
        pl.when(column == which)(functools.partial(sort_at, which))


def merge(parts, after=()):
    sub = (parts[0].shape[0] - STATS) // 4
    block = jax.ShapeDtypeStruct((2, sub, HEAD_DIM), jnp.bfloat16)
    return pl.pallas_call(
        functools.partial(merge_kernel, len(after)),
        out_shape=[block] * 4,
        in_specs=[ANY] * len(after) + [VMEM] * len(parts),
        out_specs=[VMEM] * 4,
        scratch_shapes=[pltpu.VMEM((4,) + block.shape, jnp.bfloat16)],
        compiler_params=pltpu.CompilerParams(vmem_limit_bytes=6 << 20),
        cost_estimate=pl.CostEstimate(flops=1 << 10, bytes_accessed=1 << 10, transcendentals=0),
        name="merge",
    )(*after, *parts)


def assemble_kernel(chunk, *refs):
    pieces, (out, sem) = refs[-6:-2], refs[-2:]
    column = lax.axis_index("pb")
    pairs = []
    for d, piece in enumerate(pieces):
        for half in range(2):
            pairs.append((piece.at[half], out.at[:, aligned((column ^ d) * 4 + 2 * half + chunk, HEAD_DIM)]))
    for copy in run_copies(pairs, sem):
        copy.wait()


def assemble(chunk, pieces, begun=()):
    sub = pieces[0].shape[1]
    return pl.pallas_call(
        functools.partial(assemble_kernel, chunk),
        out_shape=jax.ShapeDtypeStruct((sub, 16 * HEAD_DIM), jnp.bfloat16),
        in_specs=[ANY] * (4 + len(begun)),
        out_specs=ANY,
        scratch_shapes=[pltpu.SemaphoreType.DMA((8,))],
        input_output_aliases={0: 0} if begun else {},
        compiler_params=pltpu.CompilerParams(vmem_limit_bytes=4 << 20),
        cost_estimate=pl.CostEstimate(flops=1 << 30, bytes_accessed=32 << 20, transcendentals=0),
        name="assemble",
    )(*begun, *pieces)


def by_pairs(queries, keys, values, step_of):
    steps = step_of.reshape(-1, LANES)
    swaps = [[(i, i ^ d) for i in range(4)] for d in range(4)]

    def travel(sent, axis):
        return [lax.ppermute(piece, axis, swap) for piece, swap in zip(sent, swaps[1:])]

    order = ((0, True), (0, False), (1, True), (1, False))
    packed = pack((order[:1], order[1:]), queries, keys, values)
    got = travel(packed[:1], "ka"), travel(packed[1:2], "ka")
    moved = travel(packed[2:5], "pb"), travel(packed[5:], "pb")
    parts = []
    for i, (chunk, far) in enumerate(order):
        after = [parts[-1][0]] if parts else []
        parts.append(attend(chunk, far, max(i - 1, 0), steps, queries, keys, values, moved[min(i, 1)], got[chunk], after))
    far = [collect(lax.ppermute(same, "ka", swaps[2]), lax.ppermute(cross, "ka", swaps[3])) for same, cross in parts[::2]]
    result = ()
    blocks = ()
    for chunk, (own, beside) in enumerate(parts[1::2]):
        blocks = merge([own, lax.ppermute(beside, "ka", swaps[1]), far[chunk]], blocks[:1])
        result = (assemble(chunk, [blocks[0]] + travel(blocks[1:], "pb"), result),)
    return result[0]


def on_device(queries, keys, values, step_of):
    rows = queries.shape[0]
    held, block = keys.shape
    square = (
        lax.axis_size("pb") == 4
        and lax.axis_size("ka") == 4
        and held == rows == 4 * LANES
        and block == 4 * HEAD_DIM
    )
    if square:
        return by_pairs(queries, keys, values, step_of)
    return on_any(queries, keys, values, step_of)


def solution(mesh):
    placed = (
        P(("groups", "pb"), None),
        P(("groups", "ka"), "pb"),
        P(("groups", "ka"), "pb"),
        P("groups"),
    )
    return jax.shard_map(
        on_device,
        mesh=mesh,
        in_specs=placed,
        out_specs=P(("groups", "pb", "ka"), None),
        check_vma=False,
    )
```

```python
import functools
import math

import jax
import jax.numpy as jnp
from jax import lax
from jax.experimental import pallas as pl
from jax.experimental.pallas import tpu as pltpu
from jax.sharding import PartitionSpec as P

HEAD_DIM = 128
LANES = 128
LOW_SCORE = -1e30
UNSEEN = -float(1 << 20)
STATS = 16
PACK_VMEM = 419 << 17
ANY = pl.BlockSpec(memory_space=pl.ANY)
VMEM = pl.BlockSpec(memory_space=pltpu.VMEM)


def attend_half(q_rows, q_steps, keys_all, values_all, key_steps, block_keys):
    row_count, width = q_rows.shape
    head_size = HEAD_DIM
    head_count = width // head_size
    key_count = keys_all.shape[0]
    block_count = key_count // block_keys
    factor_scale = 1.0 / math.sqrt(head_size)
    q_heads = q_rows.reshape(row_count, head_count, head_size)
    blocks = (
        keys_all.reshape(block_count, block_keys, head_count, head_size),
        values_all.reshape(block_count, block_keys, head_count, head_size),
        key_steps.reshape(block_count, block_keys),
    )
    last_step = q_steps[row_count - 1]

    def compute(carry, key_block, value_block, step_block):
        run_max, run_sum, run_out = carry
        scores = (
            jnp.einsum("rhd,khd->hkr", q_heads, key_block, preferred_element_type=jnp.float32)
            * factor_scale
        )
        visible = step_block[None, :, None] <= q_steps[None, None, :]
        masked = jnp.where(visible, scores, LOW_SCORE)
        new_max = jnp.maximum(run_max, jnp.max(masked, axis=1))
        weights = jnp.where(visible, jnp.exp(masked - new_max[:, None, :]), 0.0)
        rescale = jnp.exp(run_max - new_max)
        new_sum = run_sum * rescale + jnp.sum(weights, axis=1)
        update = jnp.einsum(
            "hkr,khd->rhd",
            weights.astype(jnp.bfloat16),
            value_block,
            preferred_element_type=jnp.float32,
        )
        new_out = run_out * jnp.transpose(rescale)[:, :, None] + update
        return (new_max, new_sum, new_out)

    def visit(carry, block):
        key_block, value_block, step_block = block
        result = lax.cond(
            step_block[0] <= last_step,
            lambda state: compute(state, key_block, value_block, step_block),
            lambda state: state,
            carry,
        )
        return (result, None)

    initial = (
        jnp.full((head_count, row_count), LOW_SCORE, jnp.float32),
        jnp.zeros((head_count, row_count), jnp.float32),
        jnp.zeros((row_count, head_count, head_size), jnp.float32),
    )
    final_state, unused = lax.scan(visit, initial, blocks)
    return final_state


def on_any(queries, keys, values, step_of):
    block_rows, width = queries.shape
    head_size = HEAD_DIM
    head_count = width // head_size
    key_parts = lax.axis_size("ka")
    query_index = lax.axis_index("pb")
    key_index = lax.axis_index("ka")
    shard_rows = block_rows // key_parts
    half_rows = block_rows // 2
    key_count = keys.shape[0]
    first_steps = lax.dynamic_slice_in_dim(step_of, query_index * block_rows, half_rows)
    second_steps = lax.dynamic_slice_in_dim(
        step_of, query_index * block_rows + half_rows, half_rows
    )
    keys_mine, values_mine = (keys, values)
    key_steps = lax.dynamic_slice_in_dim(step_of, key_index * key_count, key_count)
    keys_all, values_all = (
        lax.all_gather(keys_mine, "pb", axis=1, tiled=True),
        lax.all_gather(values_mine, "pb", axis=1, tiled=True),
    )
    block_keys = math.gcd(64, key_count)
    first_state = attend_half(
        queries[:half_rows], first_steps, keys_all, values_all, key_steps, block_keys
    )
    second_state = attend_half(
        queries[half_rows:], second_steps, keys_all, values_all, key_steps, block_keys
    )
    row_max = jnp.concatenate([first_state[0], second_state[0]], axis=1)
    row_sum = jnp.concatenate([first_state[1], second_state[1]], axis=1)
    row_out = jnp.concatenate([first_state[2], second_state[2]], axis=0)
    sent = (
        jnp.transpose(row_max)[:, None, :],
        jnp.transpose(row_sum)[:, None, :],
        row_out.reshape(block_rows, 1, width),
    )
    got_max, got_sum, got_out = (
        lax.all_to_all(sent[0], "ka", split_axis=0, concat_axis=1, tiled=True),
        lax.all_to_all(sent[1], "ka", split_axis=0, concat_axis=1, tiled=True),
        lax.all_to_all(sent[2], "ka", split_axis=0, concat_axis=1, tiled=True),
    )
    best = jnp.max(got_max, axis=1, keepdims=True)
    weight = jnp.exp(got_max - best)
    total = jnp.sum(got_sum * weight, axis=1)
    shares = weight / total[:, None, :]
    pieces = got_out.reshape(shard_rows, key_parts, head_count, head_size) * shares[:, :, :, None]
    result = jnp.sum(pieces, axis=1).reshape(shard_rows, width)
    result = result.astype(jnp.bfloat16)
    return result

def run_copies(pairs, sem):
    copies = [pltpu.make_async_copy(a, b, sem.at[i]) for i, (a, b) in enumerate(pairs)]
    for copy in copies:
        copy.start()
    return copies


def aligned(index, size):
    return pl.ds(pl.multiple_of(index * size, size), size)


def region_of(z, far):
    return 1 - z // 2 if far else z // 2


def pack_kernel(chunks, batches, waits, queries, keys, values, *refs):
    outs, sem = refs[waits:-1], refs[-1]
    column = lax.axis_index("pb")
    z = lax.axis_index("ka")
    half = z % 2
    heads = keys.shape[1] // HEAD_DIM
    count = queries.shape[0] // 2
    pairs = []
    for chunk, to in zip(chunks, outs):
        theirs = aligned((1 - half) * 2 + chunk, HEAD_DIM)
        pairs += [(keys.at[:, theirs], to.at[0]), (values.at[:, theirs], to.at[1])]
    for (d, batch), to in zip(batches, outs[len(chunks):]):
        for i, (chunk, far) in enumerate(batch):
            cut = (aligned(region_of(z, far), count), aligned((column ^ d) * heads + half * 2 + chunk, HEAD_DIM))
            pairs.append((queries.at[cut], to.at[pl.ds(i * count, count), :]))
    for copy in run_copies(pairs, sem):
        copy.wait()


def pack(chunks, batches, queries, keys, values, after=()):
    pair = jax.ShapeDtypeStruct((2, keys.shape[0], HEAD_DIM), keys.dtype)
    rows = [jax.ShapeDtypeStruct((len(batch) * queries.shape[0] // 2, HEAD_DIM), queries.dtype) for _, batch in batches]
    return pl.pallas_call(
        functools.partial(pack_kernel, chunks, batches, len(after)),
        out_shape=[pair] * len(chunks) + rows,
        in_specs=[ANY] * (3 + len(after)),
        out_specs=[ANY] * (len(chunks) + len(batches)),
        scratch_shapes=[pltpu.SemaphoreType.DMA((2 * len(chunks) + sum(len(batch) for _, batch in batches),))],
        compiler_params=pltpu.CompilerParams(vmem_limit_bytes=PACK_VMEM),
        name="pack",
    )(queries, keys, values, *after)


def attend_kernel(chunk, far, skips, waits, scale, steps_ref, queries, keys, values, *refs):
    *moved, got, same, cross, q_buf, k_buf, v_buf = refs[waits:]
    column = lax.axis_index("pb")
    z = lax.axis_index("ka")
    half_rows = q_buf.shape[1]
    sub = half_rows // 2
    held = keys.shape[0]
    pair = 2 * held

    def sort_queries(mine):
        for d, skip, q in zip((1, 2, 3), skips, moved):
            q_buf[mine ^ d] = q[skip * half_rows:(skip + 1) * half_rows, :]

    def work(which):
        upper, half = which // 2, which % 2
        start = half_rows if far == (upper == 0) else 0
        base = upper * pair
        outs = (same, cross) if half == 0 else (cross, same)

        def own_queries(mine):
            at = (mine * 4 + half * 2 + chunk) * HEAD_DIM
            q_buf[mine] = queries[start:start + half_rows, at:at + HEAD_DIM]

        for mine in range(4):
            pl.when(column == mine)(functools.partial(own_queries, mine))
        head = slice((half * 2 + chunk) * HEAD_DIM, (half * 2 + chunk + 1) * HEAD_DIM)
        for buf, own, theirs in ((k_buf, keys, got.at[0]), (v_buf, values, got.at[1])):
            buf[half * held:(half + 1) * held, :HEAD_DIM] = own[:, head]
            buf[(1 - half) * held:(2 - half) * held, :HEAD_DIM] = theirs[...]
        v_buf[:, HEAD_DIM:] = jnp.ones((pair, HEAD_DIM), jnp.bfloat16)
        steps = steps_ref[...].astype(jnp.float32)
        columns = jnp.transpose(steps)

        def tile(slot, first_row, limit, masked_from, stats, first=0, size=half_rows):
            q = q_buf[(slot + 2 * upper) % 4, first:first + size, :]
            scores = lax.dot_general(q, k_buf[:limit, :], (((1,), (1,)), ((), ())), preferred_element_type=jnp.float32)
            if masked_from < limit:
                at = (first_row + first) // LANES
                q_steps = jnp.concatenate([columns[:, g:g + 1] for g in range(at, at + size // LANES)], axis=0)
                k_steps = jnp.concatenate(
                    [steps[g:g + 1] for g in range((base + masked_from) // LANES, (base + limit) // LANES)], axis=1)
                seen = jnp.where(k_steps <= q_steps, scores[:, masked_from:], UNSEEN / scale)
                scores = jnp.concatenate([scores[:, :masked_from], seen], axis=1) if masked_from else seen
            top = jnp.max(scores, axis=1, keepdims=True) * scale
            top = top.astype(jnp.bfloat16).astype(jnp.float32)
            weights = jnp.exp2(scores * scale - top).astype(jnp.bfloat16)
            mixed = lax.dot_general(weights, v_buf[:limit, :], (((1,), (0,)), ((), ())), preferred_element_type=jnp.float32)
            total = mixed[:, HEAD_DIM:]
            result = (mixed[:, :HEAD_DIM] / total).astype(jnp.bfloat16)
            for j in range(0, size, sub):
                outs[(first + j) // sub][slot * sub:(slot + 1) * sub, :] = result[j:j + sub]
            high = total.astype(jnp.bfloat16).astype(jnp.float32)
            lane = lax.broadcasted_iota(jnp.int32, (size, LANES), 1)
            stats = jnp.where(lane == 3 * slot, top, stats)
            stats = jnp.where(lane == 3 * slot + 1, high, stats)
            return jnp.where(lane == 3 * slot + 2, total - high, stats)

        reach = start + half_rows + LANES
        stats = jnp.zeros((half_rows, LANES), jnp.float32)
        stats = tile(0, base + start, reach, start, stats)
        stats = tile(1, base + held + start, min(held + reach, pair), held + start, stats)
        if upper == 0:
            stats = tile(2, 0, pair, pair, stats)
            stats = tile(3, 0, pair, pair, stats)
        stats = [stats[:sub], stats[sub:]]
        if upper == 1 and not far:
            stats[1] = tile(3, held + start, LANES, 0, stats[1], sub, sub)
        for out, of in zip(outs, stats):
            out[4 * sub:, :] = jnp.transpose(of)[:STATS].astype(jnp.bfloat16)

    for which in range(4):
        pl.when(column == which)(functools.partial(sort_queries, which))
    for which in range(4):
        pl.when(z == which)(functools.partial(work, which))


def attend(chunk, far, skips, steps, queries, keys, values, moved, got, after=()):
    held = keys.shape[0]
    part = jax.ShapeDtypeStruct((held + STATS, LANES), jnp.bfloat16)
    return pl.pallas_call(
        functools.partial(attend_kernel, chunk, far, skips, len(after), math.log2(math.e) / math.sqrt(HEAD_DIM)),
        out_shape=[part] * 2,
        in_specs=[VMEM] * 4 + [ANY] * len(after) + [VMEM] * 4,
        out_specs=[VMEM] * 2,
        scratch_shapes=[
            pltpu.VMEM((4, held // 2, HEAD_DIM), jnp.bfloat16),
            pltpu.VMEM((2 * held, HEAD_DIM), jnp.bfloat16),
            pltpu.VMEM((2 * held, 2 * HEAD_DIM), jnp.bfloat16),
        ],
        compiler_params=pltpu.CompilerParams(vmem_limit_bytes=24 << 20),
        cost_estimate=pl.CostEstimate(flops=1 << 10, bytes_accessed=1 << 10, transcendentals=0),
        name="attend_far" if far else "attend_near",
    )(steps, queries, keys, values, *after, *moved, *got)


def collect_kernel(a, b, out, sem):
    for copy in run_copies([(a, out.at[0]), (b, out.at[1])], sem):
        copy.wait()


def collect(a, b):
    return pl.pallas_call(
        collect_kernel,
        out_shape=jax.ShapeDtypeStruct((2,) + a.shape, a.dtype),
        in_specs=[ANY] * 2,
        out_specs=ANY,
        scratch_shapes=[pltpu.SemaphoreType.DMA((2,))],
        compiler_params=pltpu.CompilerParams(vmem_limit_bytes=4 << 20),
        cost_estimate=pl.CostEstimate(flops=1 << 30, bytes_accessed=32 << 20, transcendentals=0),
        name="collect",
    )(a, b)


def merge_kernel(waits, *refs):
    own, from_1, far = refs[waits:waits + 3]
    outs, result = refs[waits + 3:-1], refs[-1]
    column = lax.axis_index("pb")
    z = lax.axis_index("ka")
    sub = result.shape[2]
    arrived = (own, from_1, far.at[0], far.at[1])

    def merge_at(which):
        held = [arrived[which ^ s] for s in range(4)]
        stats = [jnp.transpose(held[s][4 * sub:, :].astype(jnp.float32)) for s in range(4)]

        def part(s, slot):
            return held[s][slot * sub:(slot + 1) * sub, :]

        for half in range(2):
            for block in range(4):
                if block == 0 or block == 1 and which < 3:
                    result[block, half] = part(half, block)
                    continue
                parts = ((half, block), (2 + half, (block + 2) % 4))
                tops = [stats[s][:, 3 * slot:3 * slot + 1] for s, slot in parts]
                totals = [stats[s][:, 3 * slot + 1:3 * slot + 2] + stats[s][:, 3 * slot + 2:3 * slot + 3] for s, slot in parts]
                best = jnp.maximum(*tops)
                shares = [total * jnp.exp2(top - best) for top, total in zip(tops, totals)]
                share = shares[0] / (shares[0] + shares[1])
                a, b = [part(s, slot).astype(jnp.float32) for s, slot in parts]
                result[block, half] = (a * share + b * (1.0 - share)).astype(jnp.bfloat16)

    def sort_at(which):
        for d, out in enumerate(outs):
            out[...] = result[which ^ d]

    for which in range(4):
        pl.when(z == which)(functools.partial(merge_at, which))
    for which in range(4):
        pl.when(column == which)(functools.partial(sort_at, which))


def merge(parts, after=()):
    sub = (parts[0].shape[0] - STATS) // 4
    block = jax.ShapeDtypeStruct((2, sub, HEAD_DIM), jnp.bfloat16)
    return pl.pallas_call(
        functools.partial(merge_kernel, len(after)),
        out_shape=[block] * 4,
        in_specs=[ANY] * len(after) + [VMEM] * len(parts),
        out_specs=[VMEM] * 4,
        scratch_shapes=[pltpu.VMEM((4,) + block.shape, jnp.bfloat16)],
        compiler_params=pltpu.CompilerParams(vmem_limit_bytes=6 << 20),
        cost_estimate=pl.CostEstimate(flops=1 << 10, bytes_accessed=1 << 10, transcendentals=0),
        name="merge",
    )(*after, *parts)


def assemble_kernel(chunk, *refs):
    pieces, (out, sem) = refs[-6:-2], refs[-2:]
    column = lax.axis_index("pb")
    pairs = []
    for d, piece in enumerate(pieces):
        for half in range(2):
            pairs.append((piece.at[half], out.at[:, aligned((column ^ d) * 4 + 2 * half + chunk, HEAD_DIM)]))
    for copy in run_copies(pairs, sem):
        copy.wait()


def assemble(chunk, pieces, begun=()):
    sub = pieces[0].shape[1]
    return pl.pallas_call(
        functools.partial(assemble_kernel, chunk),
        out_shape=jax.ShapeDtypeStruct((sub, 16 * HEAD_DIM), jnp.bfloat16),
        in_specs=[ANY] * (4 + len(begun)),
        out_specs=ANY,
        scratch_shapes=[pltpu.SemaphoreType.DMA((8,))],
        input_output_aliases={0: 0} if begun else {},
        compiler_params=pltpu.CompilerParams(vmem_limit_bytes=4 << 20),
        cost_estimate=pl.CostEstimate(flops=1 << 30, bytes_accessed=32 << 20, transcendentals=0),
        name="assemble",
    )(*begun, *pieces)


def by_pairs(queries, keys, values, step_of):
    steps = step_of.reshape(-1, LANES)
    swaps = [[(i, i ^ d) for i in range(4)] for d in range(4)]

    def travel(sent, axis):
        return [lax.ppermute(piece, axis, swap) for piece, swap in zip(sent, swaps[1:])]

    order = ((0, True), (0, False), (1, True), (1, False))
    batches = ((1, order), (2, order[:1]), (3, order[:1]), (2, order[1:]), (3, order[1:]))
    packed = pack((0, 1), batches, queries, keys, values)
    got = travel(packed[:1], "ka"), travel(packed[1:2], "ka")
    all_1, *others = [lax.ppermute(piece, "pb", swaps[d]) for piece, (d, _) in zip(packed[2:], batches)]
    first, rest = others[:2], others[2:]
    parts = []
    for i, (chunk, far) in enumerate(order):
        after = [parts[-1][0]] if parts else []
        arrived, skips = ([all_1, *first], (0, 0, 0)) if i == 0 else ([all_1, *rest], (i, i - 1, i - 1))
        parts.append(attend(chunk, far, skips, steps, queries, keys, values, arrived, got[chunk], after))
    far = [collect(lax.ppermute(same, "ka", swaps[2]), lax.ppermute(cross, "ka", swaps[3])) for same, cross in parts[::2]]
    result = ()
    blocks = ()
    for chunk, (own, beside) in enumerate(parts[1::2]):
        blocks = merge([own, lax.ppermute(beside, "ka", swaps[1]), far[chunk]], blocks[:1])
        result = (assemble(chunk, [blocks[0]] + travel(blocks[1:], "pb"), result),)
    return result[0]


def on_device(queries, keys, values, step_of):
    rows = queries.shape[0]
    held, block = keys.shape
    square = (
        lax.axis_size("pb") == 4
        and lax.axis_size("ka") == 4
        and held == rows == 4 * LANES
        and block == 4 * HEAD_DIM
    )
    if square:
        return by_pairs(queries, keys, values, step_of)
    return on_any(queries, keys, values, step_of)


def solution(mesh):
    placed = (
        P(("groups", "pb"), None),
        P(("groups", "ka"), "pb"),
        P(("groups", "ka"), "pb"),
        P("groups"),
    )
    return jax.shard_map(
        on_device,
        mesh=mesh,
        in_specs=placed,
        out_specs=P(("groups", "pb", "ka"), None),
        check_vma=False,
    )
```

```python
import functools
import math

import jax
import jax.numpy as jnp
from jax import lax
from jax.experimental import pallas as pl
from jax.experimental.pallas import tpu as pltpu
from jax.sharding import PartitionSpec as P

HEAD_DIM = 128
LANES = 128
LOW_SCORE = -1e30
UNSEEN = -float(1 << 20)
STATS = 16
PACK_VMEM = 419 << 17
ANY = pl.BlockSpec(memory_space=pl.ANY)
VMEM = pl.BlockSpec(memory_space=pltpu.VMEM)


def attend_half(q_rows, q_steps, keys_all, values_all, key_steps, block_keys):
    row_count, width = q_rows.shape
    head_size = HEAD_DIM
    head_count = width // head_size
    key_count = keys_all.shape[0]
    block_count = key_count // block_keys
    factor_scale = 1.0 / math.sqrt(head_size)
    q_heads = q_rows.reshape(row_count, head_count, head_size)
    blocks = (
        keys_all.reshape(block_count, block_keys, head_count, head_size),
        values_all.reshape(block_count, block_keys, head_count, head_size),
        key_steps.reshape(block_count, block_keys),
    )
    last_step = q_steps[row_count - 1]

    def compute(carry, key_block, value_block, step_block):
        run_max, run_sum, run_out = carry
        scores = (
            jnp.einsum("rhd,khd->hkr", q_heads, key_block, preferred_element_type=jnp.float32)
            * factor_scale
        )
        visible = step_block[None, :, None] <= q_steps[None, None, :]
        masked = jnp.where(visible, scores, LOW_SCORE)
        new_max = jnp.maximum(run_max, jnp.max(masked, axis=1))
        weights = jnp.where(visible, jnp.exp(masked - new_max[:, None, :]), 0.0)
        rescale = jnp.exp(run_max - new_max)
        new_sum = run_sum * rescale + jnp.sum(weights, axis=1)
        update = jnp.einsum(
            "hkr,khd->rhd",
            weights.astype(jnp.bfloat16),
            value_block,
            preferred_element_type=jnp.float32,
        )
        new_out = run_out * jnp.transpose(rescale)[:, :, None] + update
        return (new_max, new_sum, new_out)

    def visit(carry, block):
        key_block, value_block, step_block = block
        result = lax.cond(
            step_block[0] <= last_step,
            lambda state: compute(state, key_block, value_block, step_block),
            lambda state: state,
            carry,
        )
        return (result, None)

    initial = (
        jnp.full((head_count, row_count), LOW_SCORE, jnp.float32),
        jnp.zeros((head_count, row_count), jnp.float32),
        jnp.zeros((row_count, head_count, head_size), jnp.float32),
    )
    final_state, unused = lax.scan(visit, initial, blocks)
    return final_state


def on_any(queries, keys, values, step_of):
    block_rows, width = queries.shape
    head_size = HEAD_DIM
    head_count = width // head_size
    key_parts = lax.axis_size("ka")
    query_index = lax.axis_index("pb")
    key_index = lax.axis_index("ka")
    shard_rows = block_rows // key_parts
    half_rows = block_rows // 2
    key_count = keys.shape[0]
    first_steps = lax.dynamic_slice_in_dim(step_of, query_index * block_rows, half_rows)
    second_steps = lax.dynamic_slice_in_dim(
        step_of, query_index * block_rows + half_rows, half_rows
    )
    keys_mine, values_mine = (keys, values)
    key_steps = lax.dynamic_slice_in_dim(step_of, key_index * key_count, key_count)
    keys_all, values_all = (
        lax.all_gather(keys_mine, "pb", axis=1, tiled=True),
        lax.all_gather(values_mine, "pb", axis=1, tiled=True),
    )
    block_keys = math.gcd(64, key_count)
    first_state = attend_half(
        queries[:half_rows], first_steps, keys_all, values_all, key_steps, block_keys
    )
    second_state = attend_half(
        queries[half_rows:], second_steps, keys_all, values_all, key_steps, block_keys
    )
    row_max = jnp.concatenate([first_state[0], second_state[0]], axis=1)
    row_sum = jnp.concatenate([first_state[1], second_state[1]], axis=1)
    row_out = jnp.concatenate([first_state[2], second_state[2]], axis=0)
    sent = (
        jnp.transpose(row_max)[:, None, :],
        jnp.transpose(row_sum)[:, None, :],
        row_out.reshape(block_rows, 1, width),
    )
    got_max, got_sum, got_out = (
        lax.all_to_all(sent[0], "ka", split_axis=0, concat_axis=1, tiled=True),
        lax.all_to_all(sent[1], "ka", split_axis=0, concat_axis=1, tiled=True),
        lax.all_to_all(sent[2], "ka", split_axis=0, concat_axis=1, tiled=True),
    )
    best = jnp.max(got_max, axis=1, keepdims=True)
    weight = jnp.exp(got_max - best)
    total = jnp.sum(got_sum * weight, axis=1)
    shares = weight / total[:, None, :]
    pieces = got_out.reshape(shard_rows, key_parts, head_count, head_size) * shares[:, :, :, None]
    result = jnp.sum(pieces, axis=1).reshape(shard_rows, width)
    result = result.astype(jnp.bfloat16)
    return result

def run_copies(pairs, sem):
    copies = [pltpu.make_async_copy(a, b, sem.at[i]) for i, (a, b) in enumerate(pairs)]
    for copy in copies:
        copy.start()
    return copies


def aligned(index, size):
    return pl.ds(pl.multiple_of(index * size, size), size)


def region_of(z, far):
    return 1 - z // 2 if far else z // 2


def pack_kernel(chunks, batches, waits, queries, keys, values, *refs):
    outs, sem = refs[waits:-1], refs[-1]
    column = lax.axis_index("pb")
    z = lax.axis_index("ka")
    half = z % 2
    heads = keys.shape[1] // HEAD_DIM
    count = queries.shape[0] // 2
    pairs = []
    for chunk, to in zip(chunks, outs):
        theirs = aligned((1 - half) * 2 + chunk, HEAD_DIM)
        pairs += [(keys.at[:, theirs], to.at[0]), (values.at[:, theirs], to.at[1])]
    for (d, batch), to in zip(batches, outs[len(chunks):]):
        for i, (chunk, far) in enumerate(batch):
            cut = (aligned(region_of(z, far), count), aligned((column ^ d) * heads + half * 2 + chunk, HEAD_DIM))
            pairs.append((queries.at[cut], to.at[pl.ds(i * count, count), :]))
    for copy in run_copies(pairs, sem):
        copy.wait()


def pack(chunks, batches, queries, keys, values, after=()):
    pair = jax.ShapeDtypeStruct((2, keys.shape[0], HEAD_DIM), keys.dtype)
    rows = [jax.ShapeDtypeStruct((len(batch) * queries.shape[0] // 2, HEAD_DIM), queries.dtype) for _, batch in batches]
    return pl.pallas_call(
        functools.partial(pack_kernel, chunks, batches, len(after)),
        out_shape=[pair] * len(chunks) + rows,
        in_specs=[ANY] * (3 + len(after)),
        out_specs=[ANY] * (len(chunks) + len(batches)),
        scratch_shapes=[pltpu.SemaphoreType.DMA((2 * len(chunks) + sum(len(batch) for _, batch in batches),))],
        compiler_params=pltpu.CompilerParams(vmem_limit_bytes=PACK_VMEM),
        name="pack",
    )(queries, keys, values, *after)


def attend_kernel(chunk, fars, skips, waits, scale, steps_ref, queries, keys, values, *refs):
    moved, got, results, (q_buf, k_buf, v_buf) = refs[waits:waits + 3], refs[waits + 3], refs[waits + 4:-3], refs[-3:]
    column = lax.axis_index("pb")
    z = lax.axis_index("ka")
    half_rows = q_buf.shape[2]
    sub = half_rows // 2
    held = keys.shape[0]
    pair = 2 * held

    def sort_queries(mine):
        for d, skip, q in zip((1, 2, 3), skips, moved):
            for i in range(len(fars)):
                q_buf[i, mine ^ d] = q[(skip + i) * half_rows:(skip + i + 1) * half_rows, :]

    def work(which):
        upper, half = which // 2, which % 2
        base = upper * pair
        starts = [half_rows if far == (upper == 0) else 0 for far in fars]

        def own_queries(mine):
            at = (mine * 4 + half * 2 + chunk) * HEAD_DIM
            for i, start in enumerate(starts):
                q_buf[i, mine] = queries[start:start + half_rows, at:at + HEAD_DIM]

        for mine in range(4):
            pl.when(column == mine)(functools.partial(own_queries, mine))
        head = slice((half * 2 + chunk) * HEAD_DIM, (half * 2 + chunk + 1) * HEAD_DIM)
        for buf, own, theirs in ((k_buf, keys, got.at[0]), (v_buf, values, got.at[1])):
            buf[half * held:(half + 1) * held, :HEAD_DIM] = own[:, head]
            buf[(1 - half) * held:(2 - half) * held, :HEAD_DIM] = theirs[...]
        v_buf[:, HEAD_DIM:] = jnp.ones((pair, HEAD_DIM), jnp.bfloat16)
        steps = steps_ref[...].astype(jnp.float32)
        columns = jnp.transpose(steps)

        def tile(i, slot, first_row, limit, masked_from, stats, first=0, size=half_rows):
            q = q_buf[i, (slot + 2 * upper) % 4, first:first + size, :]
            scores = lax.dot_general(q, k_buf[:limit, :], (((1,), (1,)), ((), ())), preferred_element_type=jnp.float32)
            if masked_from < limit:
                at = (first_row + first) // LANES
                q_steps = jnp.concatenate([columns[:, g:g + 1] for g in range(at, at + size // LANES)], axis=0)
                k_steps = jnp.concatenate(
                    [steps[g:g + 1] for g in range((base + masked_from) // LANES, (base + limit) // LANES)], axis=1)
                seen = jnp.where(k_steps <= q_steps, scores[:, masked_from:], UNSEEN / scale)
                scores = jnp.concatenate([scores[:, :masked_from], seen], axis=1) if masked_from else seen
            top = jnp.max(scores, axis=1, keepdims=True) * scale
            top = top.astype(jnp.bfloat16).astype(jnp.float32)
            weights = jnp.exp2(scores * scale - top).astype(jnp.bfloat16)
            mixed = lax.dot_general(weights, v_buf[:limit, :], (((1,), (0,)), ((), ())), preferred_element_type=jnp.float32)
            total = mixed[:, HEAD_DIM:]
            result = (mixed[:, :HEAD_DIM] / total).astype(jnp.bfloat16)
            for j in range(0, size, sub):
                results[2 * i + ((first + j) // sub ^ half)][slot * sub:(slot + 1) * sub, :] = result[j:j + sub]
            high = total.astype(jnp.bfloat16).astype(jnp.float32)
            lane = lax.broadcasted_iota(jnp.int32, (size, LANES), 1)
            stats = jnp.where(lane == 3 * slot, top, stats)
            stats = jnp.where(lane == 3 * slot + 1, high, stats)
            return jnp.where(lane == 3 * slot + 2, total - high, stats)

        for i, (far, start) in enumerate(zip(fars, starts)):
            reach = start + half_rows + LANES
            stats = jnp.zeros((half_rows, LANES), jnp.float32)
            stats = tile(i, 0, base + start, reach, start, stats)
            stats = tile(i, 1, base + held + start, min(held + reach, pair), held + start, stats)
            if upper == 0:
                stats = tile(i, 2, 0, pair, pair, stats)
                stats = tile(i, 3, 0, pair, pair, stats)
            stats = [stats[:sub], stats[sub:]]
            if upper == 1 and not far:
                stats[1] = tile(i, 3, held + start, LANES, 0, stats[1], sub, sub)
            for j, of in enumerate(stats):
                results[2 * i + (j ^ half)][4 * sub:, :] = jnp.transpose(of)[:STATS].astype(jnp.bfloat16)

    for which in range(4):
        pl.when(column == which)(functools.partial(sort_queries, which))
    for which in range(4):
        pl.when(z == which)(functools.partial(work, which))


def attend(chunk, fars, skips, steps, queries, keys, values, moved, got, after=()):
    held = keys.shape[0]
    part = jax.ShapeDtypeStruct((held + STATS, LANES), jnp.bfloat16)
    return pl.pallas_call(
        functools.partial(attend_kernel, chunk, fars, skips, len(after), math.log2(math.e) / math.sqrt(HEAD_DIM)),
        out_shape=[part] * (2 * len(fars)),
        in_specs=[VMEM] * 4 + [ANY] * len(after) + [VMEM] * 4,
        out_specs=[VMEM] * (2 * len(fars)),
        scratch_shapes=[
            pltpu.VMEM((len(fars), 4, held // 2, HEAD_DIM), jnp.bfloat16),
            pltpu.VMEM((2 * held, HEAD_DIM), jnp.bfloat16),
            pltpu.VMEM((2 * held, 2 * HEAD_DIM), jnp.bfloat16),
        ],
        compiler_params=pltpu.CompilerParams(vmem_limit_bytes=24 << 20),
        cost_estimate=pl.CostEstimate(flops=1 << 10, bytes_accessed=1 << 10, transcendentals=0),
        name="attend_far" if fars == (True,) else "attend",
    )(steps, queries, keys, values, *after, *moved, *got)


def mark_kernel(a, b, out):
    out[...] = jnp.zeros(out.shape, out.dtype)


def mark(a, b):
    return pl.pallas_call(
        mark_kernel,
        out_shape=jax.ShapeDtypeStruct((8, LANES), jnp.float32),
        in_specs=[ANY] * 2,
        out_specs=VMEM,
        compiler_params=pltpu.CompilerParams(vmem_limit_bytes=4 << 20),
        cost_estimate=pl.CostEstimate(flops=1 << 30, bytes_accessed=32 << 20, transcendentals=0),
        name="mark",
    )(a, b)


def merge_kernel(waits, *refs):
    arrived, outs, result = refs[waits:-5], refs[-5:-1], refs[-1]
    column = lax.axis_index("pb")
    z = lax.axis_index("ka")
    sub = result.shape[2]

    def merge_at(which):
        held = [arrived[which ^ s] for s in range(4)]
        stats = [jnp.transpose(held[s][4 * sub:, :].astype(jnp.float32)) for s in range(4)]

        def part(s, slot):
            return held[s][slot * sub:(slot + 1) * sub, :]

        for half in range(2):
            for block in range(4):
                if block == 0 or block == 1 and which < 3:
                    result[block, half] = part(half, block)
                    continue
                parts = ((half, block), (2 + half, (block + 2) % 4))
                tops = [stats[s][:, 3 * slot:3 * slot + 1] for s, slot in parts]
                totals = [stats[s][:, 3 * slot + 1:3 * slot + 2] + stats[s][:, 3 * slot + 2:3 * slot + 3] for s, slot in parts]
                best = jnp.maximum(*tops)
                shares = [total * jnp.exp2(top - best) for top, total in zip(tops, totals)]
                share = shares[0] / (shares[0] + shares[1])
                a, b = [part(s, slot).astype(jnp.float32) for s, slot in parts]
                result[block, half] = (a * share + b * (1.0 - share)).astype(jnp.bfloat16)

    def sort_at(which):
        for d, out in enumerate(outs):
            out[...] = result[which ^ d]

    for which in range(4):
        pl.when(z == which)(functools.partial(merge_at, which))
    for which in range(4):
        pl.when(column == which)(functools.partial(sort_at, which))


def merge(parts, after=()):
    sub = (parts[0].shape[0] - STATS) // 4
    block = jax.ShapeDtypeStruct((2, sub, HEAD_DIM), jnp.bfloat16)
    return pl.pallas_call(
        functools.partial(merge_kernel, len(after)),
        out_shape=[block] * 4,
        in_specs=[ANY] * len(after) + [VMEM] * len(parts),
        out_specs=[VMEM] * 4,
        scratch_shapes=[pltpu.VMEM((4,) + block.shape, jnp.bfloat16)],
        compiler_params=pltpu.CompilerParams(vmem_limit_bytes=6 << 20),
        cost_estimate=pl.CostEstimate(flops=1 << 10, bytes_accessed=1 << 10, transcendentals=0),
        name="merge",
    )(*after, *parts)


def assemble_kernel(chunk, *refs):
    pieces, (out, sem) = refs[-6:-2], refs[-2:]
    column = lax.axis_index("pb")
    pairs = []
    for d, piece in enumerate(pieces):
        for half in range(2):
            pairs.append((piece.at[half], out.at[:, aligned((column ^ d) * 4 + 2 * half + chunk, HEAD_DIM)]))
    for copy in run_copies(pairs, sem):
        copy.wait()


def assemble(chunk, pieces, begun=()):
    sub = pieces[0].shape[1]
    return pl.pallas_call(
        functools.partial(assemble_kernel, chunk),
        out_shape=jax.ShapeDtypeStruct((sub, 16 * HEAD_DIM), jnp.bfloat16),
        in_specs=[ANY] * (4 + len(begun)),
        out_specs=ANY,
        scratch_shapes=[pltpu.SemaphoreType.DMA((8,))],
        input_output_aliases={0: 0} if begun else {},
        compiler_params=pltpu.CompilerParams(vmem_limit_bytes=4 << 20),
        cost_estimate=pl.CostEstimate(flops=1 << 30, bytes_accessed=32 << 20, transcendentals=0),
        name="assemble",
    )(*begun, *pieces)


def by_pairs(queries, keys, values, step_of):
    steps = step_of.reshape(-1, LANES)
    swaps = [[(i, i ^ d) for i in range(4)] for d in range(4)]

    def travel(sent, axis):
        return [lax.ppermute(piece, axis, swap) for piece, swap in zip(sent, swaps[1:])]

    order = ((0, True), (0, False), (1, True), (1, False))
    batches = ((1, order), (2, order[:1]), (3, order[:1]), (2, order[1:]), (3, order[1:]))
    packed = pack((0, 1), batches, queries, keys, values)
    got = travel(packed[:1], "ka"), travel(packed[1:2], "ka")
    all_1, *others = [lax.ppermute(piece, "pb", swaps[d]) for piece, (d, _) in zip(packed[2:], batches)]
    first, rest = others[:2], others[2:]
    def work(chunk, fars, arrived, skips, after):
        parts = attend(chunk, fars, skips, steps, queries, keys, values, arrived, got[chunk], after)
        return [parts[i:i + 2] for i in range(0, len(parts), 2)]

    parts = work(0, (True,), [all_1, *first], (0, 0, 0), [])
    parts += work(0, (False,), [all_1, *rest], (1, 0, 0), [parts[-1][0]])
    parts += work(1, (True, False), [all_1, *rest], (2, 1, 1), [parts[-1][0]])
    far = [[lax.ppermute(same, "ka", swaps[2]), lax.ppermute(cross, "ka", swaps[3])] for same, cross in parts[::2]]
    marks = [mark(*far[0])]
    result = ()
    blocks = ()
    for chunk, (own, beside) in enumerate(parts[1::2]):
        blocks = merge([own, lax.ppermute(beside, "ka", swaps[1]), *far[chunk]], [*blocks[:1], *marks[chunk:chunk + 1]])
        result = (assemble(chunk, [blocks[0]] + travel(blocks[1:], "pb"), result),)
    return result[0]


def on_device(queries, keys, values, step_of):
    rows = queries.shape[0]
    held, block = keys.shape
    square = (
        lax.axis_size("pb") == 4
        and lax.axis_size("ka") == 4
        and held == rows == 4 * LANES
        and block == 4 * HEAD_DIM
    )
    if square:
        return by_pairs(queries, keys, values, step_of)
    return on_any(queries, keys, values, step_of)


def solution(mesh):
    placed = (
        P(("groups", "pb"), None),
        P(("groups", "ka"), "pb"),
        P(("groups", "ka"), "pb"),
        P("groups"),
    )
    return jax.shard_map(
        on_device,
        mesh=mesh,
        in_specs=placed,
        out_specs=P(("groups", "pb", "ka"), None),
        check_vma=False,
    )
```

```python
import functools
import math

import jax
import jax.numpy as jnp
from jax import lax
from jax.experimental import pallas as pl
from jax.experimental.pallas import tpu as pltpu
from jax.sharding import PartitionSpec as P

HEAD_DIM = 128
LANES = 128
LOW_SCORE = -1e30
UNSEEN = -float(1 << 20)
STATS = 16
PACK_VMEM = 419 << 17
ANY = pl.BlockSpec(memory_space=pl.ANY)
VMEM = pl.BlockSpec(memory_space=pltpu.VMEM)


def attend_half(q_rows, q_steps, keys_all, values_all, key_steps, block_keys):
    row_count, width = q_rows.shape
    head_size = HEAD_DIM
    head_count = width // head_size
    key_count = keys_all.shape[0]
    block_count = key_count // block_keys
    factor_scale = 1.0 / math.sqrt(head_size)
    q_heads = q_rows.reshape(row_count, head_count, head_size)
    blocks = (
        keys_all.reshape(block_count, block_keys, head_count, head_size),
        values_all.reshape(block_count, block_keys, head_count, head_size),
        key_steps.reshape(block_count, block_keys),
    )
    last_step = q_steps[row_count - 1]

    def compute(carry, key_block, value_block, step_block):
        run_max, run_sum, run_out = carry
        scores = (
            jnp.einsum("rhd,khd->hkr", q_heads, key_block, preferred_element_type=jnp.float32)
            * factor_scale
        )
        visible = step_block[None, :, None] <= q_steps[None, None, :]
        masked = jnp.where(visible, scores, LOW_SCORE)
        new_max = jnp.maximum(run_max, jnp.max(masked, axis=1))
        weights = jnp.where(visible, jnp.exp(masked - new_max[:, None, :]), 0.0)
        rescale = jnp.exp(run_max - new_max)
        new_sum = run_sum * rescale + jnp.sum(weights, axis=1)
        update = jnp.einsum(
            "hkr,khd->rhd",
            weights.astype(jnp.bfloat16),
            value_block,
            preferred_element_type=jnp.float32,
        )
        new_out = run_out * jnp.transpose(rescale)[:, :, None] + update
        return (new_max, new_sum, new_out)

    def visit(carry, block):
        key_block, value_block, step_block = block
        result = lax.cond(
            step_block[0] <= last_step,
            lambda state: compute(state, key_block, value_block, step_block),
            lambda state: state,
            carry,
        )
        return (result, None)

    initial = (
        jnp.full((head_count, row_count), LOW_SCORE, jnp.float32),
        jnp.zeros((head_count, row_count), jnp.float32),
        jnp.zeros((row_count, head_count, head_size), jnp.float32),
    )
    final_state, unused = lax.scan(visit, initial, blocks)
    return final_state


def on_any(queries, keys, values, step_of):
    block_rows, width = queries.shape
    head_size = HEAD_DIM
    head_count = width // head_size
    key_parts = lax.axis_size("ka")
    query_index = lax.axis_index("pb")
    key_index = lax.axis_index("ka")
    shard_rows = block_rows // key_parts
    half_rows = block_rows // 2
    key_count = keys.shape[0]
    first_steps = lax.dynamic_slice_in_dim(step_of, query_index * block_rows, half_rows)
    second_steps = lax.dynamic_slice_in_dim(
        step_of, query_index * block_rows + half_rows, half_rows
    )
    keys_mine, values_mine = (keys, values)
    key_steps = lax.dynamic_slice_in_dim(step_of, key_index * key_count, key_count)
    keys_all, values_all = (
        lax.all_gather(keys_mine, "pb", axis=1, tiled=True),
        lax.all_gather(values_mine, "pb", axis=1, tiled=True),
    )
    block_keys = math.gcd(64, key_count)
    first_state = attend_half(
        queries[:half_rows], first_steps, keys_all, values_all, key_steps, block_keys
    )
    second_state = attend_half(
        queries[half_rows:], second_steps, keys_all, values_all, key_steps, block_keys
    )
    row_max = jnp.concatenate([first_state[0], second_state[0]], axis=1)
    row_sum = jnp.concatenate([first_state[1], second_state[1]], axis=1)
    row_out = jnp.concatenate([first_state[2], second_state[2]], axis=0)
    sent = (
        jnp.transpose(row_max)[:, None, :],
        jnp.transpose(row_sum)[:, None, :],
        row_out.reshape(block_rows, 1, width),
    )
    got_max, got_sum, got_out = (
        lax.all_to_all(sent[0], "ka", split_axis=0, concat_axis=1, tiled=True),
        lax.all_to_all(sent[1], "ka", split_axis=0, concat_axis=1, tiled=True),
        lax.all_to_all(sent[2], "ka", split_axis=0, concat_axis=1, tiled=True),
    )
    best = jnp.max(got_max, axis=1, keepdims=True)
    weight = jnp.exp(got_max - best)
    total = jnp.sum(got_sum * weight, axis=1)
    shares = weight / total[:, None, :]
    pieces = got_out.reshape(shard_rows, key_parts, head_count, head_size) * shares[:, :, :, None]
    result = jnp.sum(pieces, axis=1).reshape(shard_rows, width)
    result = result.astype(jnp.bfloat16)
    return result

def run_copies(pairs, sem):
    copies = [pltpu.make_async_copy(a, b, sem.at[i]) for i, (a, b) in enumerate(pairs)]
    for copy in copies:
        copy.start()
    return copies


def aligned(index, size):
    return pl.ds(pl.multiple_of(index * size, size), size)


def region_of(z, far):
    return 1 - z // 2 if far else z // 2


def pack_kernel(chunks, batches, waits, queries, keys, values, *refs):
    outs, sem = refs[waits:-1], refs[-1]
    column = lax.axis_index("pb")
    z = lax.axis_index("ka")
    half = z % 2
    heads = keys.shape[1] // HEAD_DIM
    count = queries.shape[0] // 2
    pairs = []
    for chunk, to in zip(chunks, outs):
        theirs = aligned((1 - half) * 2 + chunk, HEAD_DIM)
        pairs += [(keys.at[:, theirs], to.at[0]), (values.at[:, theirs], to.at[1])]
    for (d, batch), to in zip(batches, outs[len(chunks):]):
        for i, (chunk, far) in enumerate(batch):
            cut = (aligned(region_of(z, far), count), aligned((column ^ d) * heads + half * 2 + chunk, HEAD_DIM))
            pairs.append((queries.at[cut], to.at[pl.ds(i * count, count), :]))
    for copy in run_copies(pairs, sem):
        copy.wait()


def pack(chunks, batches, queries, keys, values, after=()):
    pair = jax.ShapeDtypeStruct((2, keys.shape[0], HEAD_DIM), keys.dtype)
    rows = [jax.ShapeDtypeStruct((len(batch) * queries.shape[0] // 2, HEAD_DIM), queries.dtype) for _, batch in batches]
    return pl.pallas_call(
        functools.partial(pack_kernel, chunks, batches, len(after)),
        out_shape=[pair] * len(chunks) + rows,
        in_specs=[ANY] * (3 + len(after)),
        out_specs=[ANY] * (len(chunks) + len(batches)),
        scratch_shapes=[pltpu.SemaphoreType.DMA((2 * len(chunks) + sum(len(batch) for _, batch in batches),))],
        compiler_params=pltpu.CompilerParams(vmem_limit_bytes=PACK_VMEM),
        name="pack",
    )(queries, keys, values, *after)


def attend_kernel(shapes, skips, waits, scale, steps_ref, queries, keys, values, *refs):
    chunks = sorted({chunk for chunk, _ in shapes})
    refs = refs[waits:]
    moved, got, results = refs[:3], refs[3:3 + len(chunks)], refs[3 + len(chunks):-3]
    q_buf, k_buf, v_buf = refs[-3:]
    column = lax.axis_index("pb")
    z = lax.axis_index("ka")
    half_rows = q_buf.shape[2]
    sub = half_rows // 2
    held = keys.shape[0]
    pair = 2 * held

    def sort_queries(mine):
        for d, skip, q in zip((1, 2, 3), skips, moved):
            for i in range(len(shapes)):
                q_buf[i, mine ^ d] = q[(skip + i) * half_rows:(skip + i + 1) * half_rows, :]

    def work(which):
        upper, half = which // 2, which % 2
        base = upper * pair
        starts = [half_rows if far == (upper == 0) else 0 for _, far in shapes]

        def own_queries(mine):
            for i, ((chunk, _), start) in enumerate(zip(shapes, starts)):
                at = (mine * 4 + half * 2 + chunk) * HEAD_DIM
                q_buf[i, mine] = queries[start:start + half_rows, at:at + HEAD_DIM]

        for mine in range(4):
            pl.when(column == mine)(functools.partial(own_queries, mine))
        for kv, chunk in enumerate(chunks):
            head = slice((half * 2 + chunk) * HEAD_DIM, (half * 2 + chunk + 1) * HEAD_DIM)
            for buf, own, theirs in ((k_buf, keys, got[kv].at[0]), (v_buf, values, got[kv].at[1])):
                buf[kv, half * held:(half + 1) * held, :HEAD_DIM] = own[:, head]
                buf[kv, (1 - half) * held:(2 - half) * held, :HEAD_DIM] = theirs[...]
            v_buf[kv, :, HEAD_DIM:] = jnp.ones((pair, HEAD_DIM), jnp.bfloat16)
        steps = steps_ref[...].astype(jnp.float32)
        columns = jnp.transpose(steps)

        def tile(i, slot, first_row, limit, masked_from, stats, first=0, size=half_rows):
            q = q_buf[i, (slot + 2 * upper) % 4, first:first + size, :]
            kv = chunks.index(shapes[i][0])
            scores = lax.dot_general(q, k_buf[kv, :limit, :], (((1,), (1,)), ((), ())), preferred_element_type=jnp.float32)
            if masked_from < limit:
                at = (first_row + first) // LANES
                q_steps = jnp.concatenate([columns[:, g:g + 1] for g in range(at, at + size // LANES)], axis=0)
                k_steps = jnp.concatenate(
                    [steps[g:g + 1] for g in range((base + masked_from) // LANES, (base + limit) // LANES)], axis=1)
                seen = jnp.where(k_steps <= q_steps, scores[:, masked_from:], UNSEEN / scale)
                scores = jnp.concatenate([scores[:, :masked_from], seen], axis=1) if masked_from else seen
            top = jnp.max(scores, axis=1, keepdims=True) * scale
            top = top.astype(jnp.bfloat16).astype(jnp.float32)
            weights = jnp.exp2(scores * scale - top).astype(jnp.bfloat16)
            mixed = lax.dot_general(weights, v_buf[kv, :limit, :], (((1,), (0,)), ((), ())), preferred_element_type=jnp.float32)
            total = mixed[:, HEAD_DIM:]
            result = (mixed[:, :HEAD_DIM] / total).astype(jnp.bfloat16)
            for j in range(0, size, sub):
                results[2 * i + ((first + j) // sub ^ half)][slot * sub:(slot + 1) * sub, :] = result[j:j + sub]
            high = total.astype(jnp.bfloat16).astype(jnp.float32)
            lane = lax.broadcasted_iota(jnp.int32, (size, LANES), 1)
            stats = jnp.where(lane == 3 * slot, top, stats)
            stats = jnp.where(lane == 3 * slot + 1, high, stats)
            return jnp.where(lane == 3 * slot + 2, total - high, stats)

        for i, ((_, far), start) in enumerate(zip(shapes, starts)):
            reach = start + half_rows + LANES
            stats = jnp.zeros((half_rows, LANES), jnp.float32)
            stats = tile(i, 0, base + start, reach, start, stats)
            stats = tile(i, 1, base + held + start, min(held + reach, pair), held + start, stats)
            if upper == 0:
                stats = tile(i, 2, 0, pair, pair, stats)
                stats = tile(i, 3, 0, pair, pair, stats)
            stats = [stats[:sub], stats[sub:]]
            if upper == 1 and not far:
                stats[1] = tile(i, 3, held + start, LANES, 0, stats[1], sub, sub)
            for j, of in enumerate(stats):
                results[2 * i + (j ^ half)][4 * sub:, :] = jnp.transpose(of)[:STATS].astype(jnp.bfloat16)

    for which in range(4):
        pl.when(column == which)(functools.partial(sort_queries, which))
    for which in range(4):
        pl.when(z == which)(functools.partial(work, which))


def attend(shapes, skips, steps, queries, keys, values, moved, got, after=()):
    held = keys.shape[0]
    part = jax.ShapeDtypeStruct((held + STATS, LANES), jnp.bfloat16)
    return pl.pallas_call(
        functools.partial(attend_kernel, shapes, skips, len(after), math.log2(math.e) / math.sqrt(HEAD_DIM)),
        out_shape=[part] * (2 * len(shapes)),
        in_specs=[VMEM] * 4 + [ANY] * len(after) + [VMEM] * (3 + len(got)),
        out_specs=[VMEM] * (2 * len(shapes)),
        scratch_shapes=[
            pltpu.VMEM((len(shapes), 4, held // 2, HEAD_DIM), jnp.bfloat16),
            pltpu.VMEM((len(got), 2 * held, HEAD_DIM), jnp.bfloat16),
            pltpu.VMEM((len(got), 2 * held, 2 * HEAD_DIM), jnp.bfloat16),
        ],
        compiler_params=pltpu.CompilerParams(vmem_limit_bytes=24 << 20),
        cost_estimate=pl.CostEstimate(flops=1 << 10, bytes_accessed=1 << 10, transcendentals=0),
        name="attend_first" if len(shapes) == 1 else "attend_rest",
    )(steps, queries, keys, values, *after, *moved, *got)


def mark_kernel(a, b, out):
    out[...] = jnp.zeros(out.shape, out.dtype)


def mark(a, b):
    return pl.pallas_call(
        mark_kernel,
        out_shape=jax.ShapeDtypeStruct((8, LANES), jnp.float32),
        in_specs=[ANY] * 2,
        out_specs=VMEM,
        compiler_params=pltpu.CompilerParams(vmem_limit_bytes=4 << 20),
        cost_estimate=pl.CostEstimate(flops=1 << 34, bytes_accessed=512 << 20, transcendentals=0),
        name="mark",
    )(a, b)


def merge_kernel(waits, *refs):
    arrived, outs, result = refs[waits:-5], refs[-5:-1], refs[-1]
    column = lax.axis_index("pb")
    z = lax.axis_index("ka")
    sub = result.shape[2]

    def merge_at(which):
        held = [arrived[which ^ s] for s in range(4)]
        stats = [jnp.transpose(held[s][4 * sub:, :].astype(jnp.float32)) for s in range(4)]

        def part(s, slot):
            return held[s][slot * sub:(slot + 1) * sub, :]

        for half in range(2):
            for block in range(4):
                if block == 0 or block == 1 and which < 3:
                    result[block, half] = part(half, block)
                    continue
                parts = ((half, block), (2 + half, (block + 2) % 4))
                tops = [stats[s][:, 3 * slot:3 * slot + 1] for s, slot in parts]
                totals = [stats[s][:, 3 * slot + 1:3 * slot + 2] + stats[s][:, 3 * slot + 2:3 * slot + 3] for s, slot in parts]
                best = jnp.maximum(*tops)
                shares = [total * jnp.exp2(top - best) for top, total in zip(tops, totals)]
                share = shares[0] / (shares[0] + shares[1])
                a, b = [part(s, slot).astype(jnp.float32) for s, slot in parts]
                result[block, half] = (a * share + b * (1.0 - share)).astype(jnp.bfloat16)

    def sort_at(which):
        for d, out in enumerate(outs):
            out[...] = result[which ^ d]

    for which in range(4):
        pl.when(z == which)(functools.partial(merge_at, which))
    for which in range(4):
        pl.when(column == which)(functools.partial(sort_at, which))


def merge(parts, after=()):
    sub = (parts[0].shape[0] - STATS) // 4
    block = jax.ShapeDtypeStruct((2, sub, HEAD_DIM), jnp.bfloat16)
    return pl.pallas_call(
        functools.partial(merge_kernel, len(after)),
        out_shape=[block] * 4,
        in_specs=[ANY] * len(after) + [VMEM] * len(parts),
        out_specs=[VMEM] * 4,
        scratch_shapes=[pltpu.VMEM((4,) + block.shape, jnp.bfloat16)],
        compiler_params=pltpu.CompilerParams(vmem_limit_bytes=6 << 20),
        cost_estimate=pl.CostEstimate(flops=1 << 10, bytes_accessed=1 << 10, transcendentals=0),
        name="merge",
    )(*after, *parts)


def assemble_kernel(chunk, *refs):
    pieces, (out, sem) = refs[-6:-2], refs[-2:]
    column = lax.axis_index("pb")
    pairs = []
    for d, piece in enumerate(pieces):
        for half in range(2):
            pairs.append((piece.at[half], out.at[:, aligned((column ^ d) * 4 + 2 * half + chunk, HEAD_DIM)]))
    for copy in run_copies(pairs, sem):
        copy.wait()


def assemble(chunk, pieces, begun=()):
    sub = pieces[0].shape[1]
    return pl.pallas_call(
        functools.partial(assemble_kernel, chunk),
        out_shape=jax.ShapeDtypeStruct((sub, 16 * HEAD_DIM), jnp.bfloat16),
        in_specs=[ANY] * (4 + len(begun)),
        out_specs=ANY,
        scratch_shapes=[pltpu.SemaphoreType.DMA((8,))],
        input_output_aliases={0: 0} if begun else {},
        compiler_params=pltpu.CompilerParams(vmem_limit_bytes=4 << 20),
        cost_estimate=pl.CostEstimate(flops=1 << 30, bytes_accessed=32 << 20, transcendentals=0),
        name="assemble",
    )(*begun, *pieces)


def by_pairs(queries, keys, values, step_of):
    steps = step_of.reshape(-1, LANES)
    swaps = [[(i, i ^ d) for i in range(4)] for d in range(4)]

    def travel(sent, axis):
        return [lax.ppermute(piece, axis, swap) for piece, swap in zip(sent, swaps[1:])]

    order = ((0, True), (0, False), (1, True), (1, False))
    batches = ((1, order), (2, order[:1]), (3, order[:1]), (2, order[1:]), (3, order[1:]))
    packed = pack((0, 1), batches, queries, keys, values)
    got = travel(packed[:1], "ka"), travel(packed[1:2], "ka")
    all_1, *others = [lax.ppermute(piece, "pb", swaps[d]) for piece, (d, _) in zip(packed[2:], batches)]
    first, rest = others[:2], others[2:]
    def work(shapes, arrived, skips, got, after=()):
        parts = attend(shapes, skips, steps, queries, keys, values, arrived, got, after)
        return [parts[i:i + 2] for i in range(0, len(parts), 2)]

    got = [pair for pairs in got for pair in pairs]
    parts = work(order[:1], [all_1, *first], (0, 0, 0), got[:1])
    parts += work(order[1:], [all_1, *rest], (1, 0, 0), got, parts[0][:1])
    far = [[lax.ppermute(same, "ka", swaps[2]), lax.ppermute(cross, "ka", swaps[3])] for same, cross in parts[::2]]
    marks = [mark(*far[0])]
    result = ()
    blocks = ()
    for chunk, (own, beside) in enumerate(parts[1::2]):
        blocks = merge([own, lax.ppermute(beside, "ka", swaps[1]), *far[chunk]], [*blocks[:1], *marks[chunk:chunk + 1]])
        result = (assemble(chunk, [blocks[0]] + travel(blocks[1:], "pb"), result),)
    return result[0]


def on_device(queries, keys, values, step_of):
    rows = queries.shape[0]
    held, block = keys.shape
    square = (
        lax.axis_size("pb") == 4
        and lax.axis_size("ka") == 4
        and held == rows == 4 * LANES
        and block == 4 * HEAD_DIM
    )
    if square:
        return by_pairs(queries, keys, values, step_of)
    return on_any(queries, keys, values, step_of)


def solution(mesh):
    placed = (
        P(("groups", "pb"), None),
        P(("groups", "ka"), "pb"),
        P(("groups", "ka"), "pb"),
        P("groups"),
    )
    return jax.shard_map(
        on_device,
        mesh=mesh,
        in_specs=placed,
        out_specs=P(("groups", "pb", "ka"), None),
        check_vma=False,
    )
```

```python
import functools
import math

import jax
import jax.numpy as jnp
from jax import lax
from jax.experimental import pallas as pl
from jax.experimental.pallas import tpu as pltpu
from jax.sharding import PartitionSpec as P

HEAD_DIM = 128
LANES = 128
LOW_SCORE = -1e30
UNSEEN = -float(1 << 20)
STATS = 16
PACK_VMEM = 419 << 17
ANY = pl.BlockSpec(memory_space=pl.ANY)
VMEM = pl.BlockSpec(memory_space=pltpu.VMEM)


def attend_half(q_rows, q_steps, keys_all, values_all, key_steps, block_keys):
    row_count, width = q_rows.shape
    head_size = HEAD_DIM
    head_count = width // head_size
    key_count = keys_all.shape[0]
    block_count = key_count // block_keys
    factor_scale = 1.0 / math.sqrt(head_size)
    q_heads = q_rows.reshape(row_count, head_count, head_size)
    blocks = (
        keys_all.reshape(block_count, block_keys, head_count, head_size),
        values_all.reshape(block_count, block_keys, head_count, head_size),
        key_steps.reshape(block_count, block_keys),
    )
    last_step = q_steps[row_count - 1]

    def compute(carry, key_block, value_block, step_block):
        run_max, run_sum, run_out = carry
        scores = (
            jnp.einsum("rhd,khd->hkr", q_heads, key_block, preferred_element_type=jnp.float32)
            * factor_scale
        )
        visible = step_block[None, :, None] <= q_steps[None, None, :]
        masked = jnp.where(visible, scores, LOW_SCORE)
        new_max = jnp.maximum(run_max, jnp.max(masked, axis=1))
        weights = jnp.where(visible, jnp.exp(masked - new_max[:, None, :]), 0.0)
        rescale = jnp.exp(run_max - new_max)
        new_sum = run_sum * rescale + jnp.sum(weights, axis=1)
        update = jnp.einsum(
            "hkr,khd->rhd",
            weights.astype(jnp.bfloat16),
            value_block,
            preferred_element_type=jnp.float32,
        )
        new_out = run_out * jnp.transpose(rescale)[:, :, None] + update
        return (new_max, new_sum, new_out)

    def visit(carry, block):
        key_block, value_block, step_block = block
        result = lax.cond(
            step_block[0] <= last_step,
            lambda state: compute(state, key_block, value_block, step_block),
            lambda state: state,
            carry,
        )
        return (result, None)

    initial = (
        jnp.full((head_count, row_count), LOW_SCORE, jnp.float32),
        jnp.zeros((head_count, row_count), jnp.float32),
        jnp.zeros((row_count, head_count, head_size), jnp.float32),
    )
    final_state, unused = lax.scan(visit, initial, blocks)
    return final_state


def on_any(queries, keys, values, step_of):
    block_rows, width = queries.shape
    head_size = HEAD_DIM
    head_count = width // head_size
    key_parts = lax.axis_size("ka")
    query_index = lax.axis_index("pb")
    key_index = lax.axis_index("ka")
    shard_rows = block_rows // key_parts
    half_rows = block_rows // 2
    key_count = keys.shape[0]
    first_steps = lax.dynamic_slice_in_dim(step_of, query_index * block_rows, half_rows)
    second_steps = lax.dynamic_slice_in_dim(
        step_of, query_index * block_rows + half_rows, half_rows
    )
    keys_mine, values_mine = (keys, values)
    key_steps = lax.dynamic_slice_in_dim(step_of, key_index * key_count, key_count)
    keys_all, values_all = (
        lax.all_gather(keys_mine, "pb", axis=1, tiled=True),
        lax.all_gather(values_mine, "pb", axis=1, tiled=True),
    )
    block_keys = math.gcd(64, key_count)
    first_state = attend_half(
        queries[:half_rows], first_steps, keys_all, values_all, key_steps, block_keys
    )
    second_state = attend_half(
        queries[half_rows:], second_steps, keys_all, values_all, key_steps, block_keys
    )
    row_max = jnp.concatenate([first_state[0], second_state[0]], axis=1)
    row_sum = jnp.concatenate([first_state[1], second_state[1]], axis=1)
    row_out = jnp.concatenate([first_state[2], second_state[2]], axis=0)
    sent = (
        jnp.transpose(row_max)[:, None, :],
        jnp.transpose(row_sum)[:, None, :],
        row_out.reshape(block_rows, 1, width),
    )
    got_max, got_sum, got_out = (
        lax.all_to_all(sent[0], "ka", split_axis=0, concat_axis=1, tiled=True),
        lax.all_to_all(sent[1], "ka", split_axis=0, concat_axis=1, tiled=True),
        lax.all_to_all(sent[2], "ka", split_axis=0, concat_axis=1, tiled=True),
    )
    best = jnp.max(got_max, axis=1, keepdims=True)
    weight = jnp.exp(got_max - best)
    total = jnp.sum(got_sum * weight, axis=1)
    shares = weight / total[:, None, :]
    pieces = got_out.reshape(shard_rows, key_parts, head_count, head_size) * shares[:, :, :, None]
    result = jnp.sum(pieces, axis=1).reshape(shard_rows, width)
    result = result.astype(jnp.bfloat16)
    return result

def run_copies(pairs, sem):
    copies = [pltpu.make_async_copy(a, b, sem.at[i]) for i, (a, b) in enumerate(pairs)]
    for copy in copies:
        copy.start()
    return copies


def aligned(index, size):
    return pl.ds(pl.multiple_of(index * size, size), size)


def region_of(z, far):
    return 1 - z // 2 if far else z // 2


def pack_kernel(chunks, batches, waits, queries, keys, values, *refs):
    outs, sem = refs[waits:-1], refs[-1]
    column = lax.axis_index("pb")
    z = lax.axis_index("ka")
    half = z % 2
    heads = keys.shape[1] // HEAD_DIM
    count = queries.shape[0] // 2
    pairs = []
    for chunk, to in zip(chunks, outs):
        theirs = aligned((1 - half) * 2 + chunk, HEAD_DIM)
        pairs += [(keys.at[:, theirs], to.at[0]), (values.at[:, theirs], to.at[1])]
    for (d, batch), to in zip(batches, outs[len(chunks):]):
        for i, (chunk, far) in enumerate(batch):
            cut = (aligned(region_of(z, far), count), aligned((column ^ d) * heads + half * 2 + chunk, HEAD_DIM))
            pairs.append((queries.at[cut], to.at[pl.ds(i * count, count), :]))
    for copy in run_copies(pairs, sem):
        copy.wait()


def pack(chunks, batches, queries, keys, values, after=()):
    pair = jax.ShapeDtypeStruct((2, keys.shape[0], HEAD_DIM), keys.dtype)
    rows = [jax.ShapeDtypeStruct((len(batch) * queries.shape[0] // 2, HEAD_DIM), queries.dtype) for _, batch in batches]
    return pl.pallas_call(
        functools.partial(pack_kernel, chunks, batches, len(after)),
        out_shape=[pair] * len(chunks) + rows,
        in_specs=[ANY] * (3 + len(after)),
        out_specs=[ANY] * (len(chunks) + len(batches)),
        scratch_shapes=[pltpu.SemaphoreType.DMA((2 * len(chunks) + sum(len(batch) for _, batch in batches),))],
        compiler_params=pltpu.CompilerParams(vmem_limit_bytes=PACK_VMEM),
        name="pack",
    )(queries, keys, values, *after)


def attend_kernel(chunk, fars, skips, waits, scale, steps_ref, queries, keys, values, *refs):
    moved, got, results, (q_buf, k_buf, v_buf) = refs[waits:waits + 3], refs[waits + 3], refs[waits + 4:-3], refs[-3:]
    column = lax.axis_index("pb")
    z = lax.axis_index("ka")
    half_rows = q_buf.shape[2]
    sub = half_rows // 2
    held = keys.shape[0]
    pair = 2 * held

    def sort_queries(mine):
        for d, skip, q in zip((1, 2, 3), skips, moved):
            for i in range(len(fars)):
                q_buf[i, mine ^ d] = q[(skip + i) * half_rows:(skip + i + 1) * half_rows, :]

    def work(which):
        upper, half = which // 2, which % 2
        base = upper * pair
        starts = [half_rows if far == (upper == 0) else 0 for far in fars]

        def own_queries(mine):
            at = (mine * 4 + half * 2 + chunk) * HEAD_DIM
            for i, start in enumerate(starts):
                q_buf[i, mine] = queries[start:start + half_rows, at:at + HEAD_DIM]

        for mine in range(4):
            pl.when(column == mine)(functools.partial(own_queries, mine))
        head = slice((half * 2 + chunk) * HEAD_DIM, (half * 2 + chunk + 1) * HEAD_DIM)
        for buf, own, theirs in ((k_buf, keys, got.at[0]), (v_buf, values, got.at[1])):
            buf[half * held:(half + 1) * held, :HEAD_DIM] = own[:, head]
            buf[(1 - half) * held:(2 - half) * held, :HEAD_DIM] = theirs[...]
        v_buf[:, HEAD_DIM:] = jnp.ones((pair, HEAD_DIM), jnp.bfloat16)
        steps = steps_ref[...].astype(jnp.float32)
        columns = jnp.transpose(steps)

        def tile(i, slot, first_row, limit, masked_from, stats, first=0, size=half_rows):
            q = q_buf[i, (slot + 2 * upper) % 4, first:first + size, :]
            scores = lax.dot_general(q, k_buf[:limit, :], (((1,), (1,)), ((), ())), preferred_element_type=jnp.float32)
            if masked_from < limit:
                at = (first_row + first) // LANES
                q_steps = jnp.concatenate([columns[:, g:g + 1] for g in range(at, at + size // LANES)], axis=0)
                k_steps = jnp.concatenate(
                    [steps[g:g + 1] for g in range((base + masked_from) // LANES, (base + limit) // LANES)], axis=1)
                seen = jnp.where(k_steps <= q_steps, scores[:, masked_from:], UNSEEN / scale)
                scores = jnp.concatenate([scores[:, :masked_from], seen], axis=1) if masked_from else seen
            top = jnp.max(scores, axis=1, keepdims=True) * scale
            top = top.astype(jnp.bfloat16).astype(jnp.float32)
            weights = jnp.exp2(scores * scale - top).astype(jnp.bfloat16)
            mixed = lax.dot_general(weights, v_buf[:limit, :], (((1,), (0,)), ((), ())), preferred_element_type=jnp.float32)
            total = mixed[:, HEAD_DIM:]
            result = (mixed[:, :HEAD_DIM] / total).astype(jnp.bfloat16)
            for j in range(0, size, sub):
                results[2 * i + ((first + j) // sub ^ half)][slot * sub:(slot + 1) * sub, :] = result[j:j + sub]
            high = total.astype(jnp.bfloat16).astype(jnp.float32)
            lane = lax.broadcasted_iota(jnp.int32, (size, LANES), 1)
            stats = jnp.where(lane == 3 * slot, top, stats)
            stats = jnp.where(lane == 3 * slot + 1, high, stats)
            return jnp.where(lane == 3 * slot + 2, total - high, stats)

        for i, (far, start) in enumerate(zip(fars, starts)):
            reach = start + half_rows + LANES
            stats = jnp.zeros((half_rows, LANES), jnp.float32)
            stats = tile(i, 0, base + start, reach, start, stats)
            stats = tile(i, 1, base + held + start, min(held + reach, pair), held + start, stats)
            if upper == 0:
                stats = tile(i, 2, 0, pair, pair, stats)
                stats = tile(i, 3, 0, pair, pair, stats)
            stats = [stats[:sub], stats[sub:]]
            if upper == 1 and not far:
                stats[1] = tile(i, 3, held + start, LANES, 0, stats[1], sub, sub)
            for j, of in enumerate(stats):
                results[2 * i + (j ^ half)][4 * sub:, :] = jnp.transpose(of)[:STATS].astype(jnp.bfloat16)

    for which in range(4):
        pl.when(column == which)(functools.partial(sort_queries, which))
    for which in range(4):
        pl.when(z == which)(functools.partial(work, which))


def attend(chunk, fars, skips, steps, queries, keys, values, moved, got, after=()):
    held = keys.shape[0]
    part = jax.ShapeDtypeStruct((held + STATS, LANES), jnp.bfloat16)
    return pl.pallas_call(
        functools.partial(attend_kernel, chunk, fars, skips, len(after), math.log2(math.e) / math.sqrt(HEAD_DIM)),
        out_shape=[part] * (2 * len(fars)),
        in_specs=[VMEM] * 4 + [ANY] * len(after) + [VMEM] * 4,
        out_specs=[VMEM] * (2 * len(fars)),
        scratch_shapes=[
            pltpu.VMEM((len(fars), 4, held // 2, HEAD_DIM), jnp.bfloat16),
            pltpu.VMEM((2 * held, HEAD_DIM), jnp.bfloat16),
            pltpu.VMEM((2 * held, 2 * HEAD_DIM), jnp.bfloat16),
        ],
        compiler_params=pltpu.CompilerParams(vmem_limit_bytes=24 << 20),
        cost_estimate=pl.CostEstimate(flops=1 << 10, bytes_accessed=1 << 10, transcendentals=0),
        name="attend_far" if fars == (True,) else "attend",
    )(steps, queries, keys, values, *after, *moved, *got)


def mark_kernel(a, b, out):
    out[...] = jnp.zeros(out.shape, out.dtype)


def mark(a, b):
    return pl.pallas_call(
        mark_kernel,
        out_shape=jax.ShapeDtypeStruct((8, LANES), jnp.float32),
        in_specs=[ANY] * 2,
        out_specs=VMEM,
        compiler_params=pltpu.CompilerParams(vmem_limit_bytes=4 << 20),
        cost_estimate=pl.CostEstimate(flops=1 << 30, bytes_accessed=32 << 20, transcendentals=0),
        name="mark",
    )(a, b)


def merge_kernel(waits, *refs):
    arrived, outs, result = refs[waits:-5], refs[-5:-1], refs[-1]
    column = lax.axis_index("pb")
    z = lax.axis_index("ka")
    sub = result.shape[2]

    def merge_at(which):
        held = [arrived[which ^ s] for s in range(4)]
        stats = [jnp.transpose(held[s][4 * sub:, :].astype(jnp.float32)) for s in range(4)]

        def part(s, slot):
            return held[s][slot * sub:(slot + 1) * sub, :]

        for half in range(2):
            for block in range(4):
                if block == 0 or block == 1 and which < 3:
                    result[block, half] = part(half, block)
                    continue
                parts = ((half, block), (2 + half, (block + 2) % 4))
                tops = [stats[s][:, 3 * slot:3 * slot + 1] for s, slot in parts]
                totals = [stats[s][:, 3 * slot + 1:3 * slot + 2] + stats[s][:, 3 * slot + 2:3 * slot + 3] for s, slot in parts]
                best = jnp.maximum(*tops)
                shares = [total * jnp.exp2(top - best) for top, total in zip(tops, totals)]
                share = shares[0] / (shares[0] + shares[1])
                a, b = [part(s, slot).astype(jnp.float32) for s, slot in parts]
                result[block, half] = (a * share + b * (1.0 - share)).astype(jnp.bfloat16)

    def sort_at(which):
        for d, out in enumerate(outs):
            out[...] = result[which ^ d]

    for which in range(4):
        pl.when(z == which)(functools.partial(merge_at, which))
    for which in range(4):
        pl.when(column == which)(functools.partial(sort_at, which))


def merge(parts, after=()):
    sub = (parts[0].shape[0] - STATS) // 4
    block = jax.ShapeDtypeStruct((2, sub, HEAD_DIM), jnp.bfloat16)
    return pl.pallas_call(
        functools.partial(merge_kernel, len(after)),
        out_shape=[block] * 4,
        in_specs=[ANY] * len(after) + [VMEM] * len(parts),
        out_specs=[VMEM] * 4,
        scratch_shapes=[pltpu.VMEM((4,) + block.shape, jnp.bfloat16)],
        compiler_params=pltpu.CompilerParams(vmem_limit_bytes=6 << 20),
        cost_estimate=pl.CostEstimate(flops=1 << 10, bytes_accessed=1 << 10, transcendentals=0),
        name="merge",
    )(*after, *parts)


def assemble_kernel(chunk, *refs):
    pieces, (out, sem) = refs[-6:-2], refs[-2:]
    column = lax.axis_index("pb")
    pairs = []
    for d, piece in zip((3, 2, 1, 0), pieces):
        for half in range(2):
            pairs.append((piece.at[half], out.at[:, aligned((column ^ d) * 4 + 2 * half + chunk, HEAD_DIM)]))
    for copy in run_copies(pairs, sem):
        copy.wait()


def assemble(chunk, pieces, begun=()):
    sub = pieces[0].shape[1]
    return pl.pallas_call(
        functools.partial(assemble_kernel, chunk),
        out_shape=jax.ShapeDtypeStruct((sub, 16 * HEAD_DIM), jnp.bfloat16),
        in_specs=[ANY] * (4 + len(begun)),
        out_specs=ANY,
        scratch_shapes=[pltpu.SemaphoreType.DMA((8,))],
        input_output_aliases={0: 0} if begun else {},
        compiler_params=pltpu.CompilerParams(vmem_limit_bytes=4 << 20),
        cost_estimate=pl.CostEstimate(flops=1 << 30, bytes_accessed=32 << 20, transcendentals=0),
        name="assemble",
    )(*begun, *pieces)


def by_pairs(queries, keys, values, step_of):
    steps = step_of.reshape(-1, LANES)
    swaps = [[(i, i ^ d) for i in range(4)] for d in range(4)]

    def travel(sent, axis):
        return [lax.ppermute(piece, axis, swap) for piece, swap in zip(sent, swaps[1:])]

    order = ((0, True), (0, False), (1, True), (1, False))
    batches = ((1, order), (2, order[:1]), (3, order[:1]), (2, order[1:]), (3, order[1:]))
    packed = pack((0, 1), batches, queries, keys, values)
    got = travel(packed[:1], "ka"), travel(packed[1:2], "ka")
    all_1, *others = [lax.ppermute(piece, "pb", swaps[d]) for piece, (d, _) in zip(packed[2:], batches)]
    first, rest = others[:2], others[2:]
    def work(chunk, fars, arrived, skips, after):
        parts = attend(chunk, fars, skips, steps, queries, keys, values, arrived, got[chunk], after)
        return [parts[i:i + 2] for i in range(0, len(parts), 2)]

    parts = work(0, (True,), [all_1, *first], (0, 0, 0), [])
    parts += work(0, (False,), [all_1, *rest], (1, 0, 0), [parts[-1][0]])
    parts += work(1, (True, False), [all_1, *rest], (2, 1, 1), [parts[-1][0]])
    far = [[lax.ppermute(same, "ka", swaps[2]), lax.ppermute(cross, "ka", swaps[3])] for same, cross in parts[::2]]
    marks = [mark(*far[0])]
    result = ()
    blocks = ()
    for chunk, (own, beside) in enumerate(parts[1::2]):
        blocks = merge([own, lax.ppermute(beside, "ka", swaps[1]), *far[chunk]], [*blocks[:1], *marks[chunk:chunk + 1]])
        others = [lax.ppermute(blocks[d], "pb", swaps[d]) for d in (3, 2, 1)]
        result = (assemble(chunk, others + [blocks[0]], result),)
    return result[0]


def on_device(queries, keys, values, step_of):
    rows = queries.shape[0]
    held, block = keys.shape
    square = (
        lax.axis_size("pb") == 4
        and lax.axis_size("ka") == 4
        and held == rows == 4 * LANES
        and block == 4 * HEAD_DIM
    )
    if square:
        return by_pairs(queries, keys, values, step_of)
    return on_any(queries, keys, values, step_of)


def solution(mesh):
    placed = (
        P(("groups", "pb"), None),
        P(("groups", "ka"), "pb"),
        P(("groups", "ka"), "pb"),
        P("groups"),
    )
    return jax.shard_map(
        on_device,
        mesh=mesh,
        in_specs=placed,
        out_specs=P(("groups", "pb", "ka"), None),
        check_vma=False,
    )
```
